32 devices in a mesh: dp: 4 (over z), seq: 2 (over core), heads: 4 (over y, x).
Axes of the slice: x: 2, y: 2, z: 4, core: 2. Of those that a mesh axis runs over, the one named last changes fastest.
Arguments:
- inputs: bfloat16 [2, 4, 1024, 1024], P(None, 'dp', ('seq', 'heads')), may hold values from -6 to 6
- w_qkv: bfloat16 [3, 1024, 1024], P(None, ('dp', 'seq'), 'heads'), may hold values from -0.1875 to 0.1875
- b_qv: bfloat16 [2, 16, 64], P(None, 'heads', ('dp', 'seq')), may hold values from -3 to 3
- w_out: bfloat16 [1024, 1024], P('heads', ('dp', 'seq')), may hold values from -3 to 3
- w_up: bfloat16 [1024, 4096], P(('dp', 'seq'), 'heads'), may hold values from -0.1875 to 0.1875
- b_up: bfloat16 [64, 64], P('heads', ('dp', 'seq')), may hold values from -3 to 3
- w_down: bfloat16 [4096, 1024], P('heads', ('dp', 'seq')), may hold values from -0.09375 to 0.09375
- ln_gains: bfloat16 [2, 1024], P(None, ('dp', 'seq')), may hold values from 0.5 to 1.5
- ln_shifts: bfloat16 [4, 1024], P(None, ('dp', 'seq')), may hold values from -2 to 2
- cotangent: bfloat16 [2, 4, 1024, 1024], P(None, 'dp', ('seq', 'heads')), may hold values from -6 to 6
Outputs:
- output: bfloat16 [2, 4, 1024, 1024], P(None, 'dp', ('seq', 'heads'))
- grad_inputs: bfloat16 [2, 4, 1024, 1024], P(None, 'dp', ('seq', 'heads'))
- grad_qkv: float32 [3, 1024, 1024], P(None, ('dp', 'seq'), 'heads')
- grad_bqv: float32 [2, 16, 64], P(None, 'heads', ('dp', 'seq'))
- grad_out: float32 [1024, 1024], P('heads', ('dp', 'seq'))
- grad_up: float32 [1024, 4096], P(('dp', 'seq'), 'heads')
- grad_bup: float32 [64, 64], P('heads', ('dp', 'seq'))
- grad_down: float32 [4096, 1024], P('heads', ('dp', 'seq'))
- grad_gains: float32 [2, 1024], P(None, ('dp', 'seq'))
- grad_shifts: float32 [4, 1024], P(None, ('dp', 'seq'))
The draws below stay inside these ranges and needn't reach their ends.
All inputs are finite; a program needn't handle non-finite values.
Results may differ from the reference program's by a relative error of at most 0.02.
Values may be sent and summed in bfloat16 or wider, within the bound.
A program may use at most 64 MiB of HBM per device.

```python
import jax
import jax.numpy as jnp
from jax import lax

D = 1024
HEADS = 16
HD = 64
FF = 4096
LEN = 1024
MB = 2
SEQS = 4


def block_scale(stream_key, shape, shards, least, top_value):
    def one(position, shards_of):
        draws = jax.random.uniform(jax.random.fold_in(jax.random.fold_in(stream_key, 6), position), (shards_of,), jnp.float32, least / len(shards), top_value / len(shards))
        return jnp.repeat(jnp.exp(draws), shape[position] // shards_of).reshape((-1,) + (1,) * (len(shape) - position - 1))

    level = one(*shards[0])
    for cut in shards[1:]:
        level = level * one(*cut)
    return level


def noise(stream_key, dims, scale, limit, shards=(), kind=jnp.bfloat16):
    array = jax.random.normal(stream_key, dims, jnp.float32) * scale
    if len(shards) > 0:
        array = block_scale(stream_key, dims, shards, -0.22, 0.18) * array
    return jnp.clip(array, min=-limit, max=limit).astype(kind)


def setup_inputs(seed: int = 0) -> dict:
    arg_keys = jax.random.split(jax.random.key(seed), 11)
    return {
        "inputs": noise(arg_keys[0], (MB, SEQS, LEN, D), 1.0, 6.0, ((1, 4), (2, 8))),
        "w_qkv": noise(arg_keys[1], (3, D, D), D ** -0.5, 0.1875, ((1, 8), (2, 4))),
        "b_qv": noise(arg_keys[2], (2, HEADS, HD), 0.5, 3.0, ((1, 4), (2, 8))),
        "w_out": noise(arg_keys[3], (D, D), (max(4, 2 * D // LEN)) ** -0.5, 3.0, ((0, 4), (1, 8))),
        "w_up": noise(arg_keys[4], (D, FF), D ** -0.5, 0.1875, ((0, 8), (1, 4))),
        "b_up": noise(arg_keys[5], (FF // HD, HD), 0.5, 3.0, ((0, 4), (1, 8))),
        "w_down": noise(arg_keys[6], (FF, D), FF ** -0.5, 0.09375, ((0, 4), (1, 8))),
        "ln_gains": jnp.clip(1.0 + 0.1 * jax.random.normal(arg_keys[7], (2, D), jnp.float32), 0.5, 1.5).astype(jnp.bfloat16),
        "ln_shifts": noise(arg_keys[8], (4, D), 0.3, 2.0, ((1, 8),)),
        "cotangent": noise(arg_keys[9], (MB, SEQS, LEN, D), 1.0, 6.0, ((1, 4), (2, 8))),
    }


EPSILON = 1e-05

@jax.custom_vjp
def low(v):
    return lax.optimization_barrier(v.astype(jnp.bfloat16)).astype(jnp.float32)

@jax.custom_vjp
def low_back(v):
    return v

def low_keep(v):
    return (low(v), None)

def low_pass(kept, grad):
    return (grad,)

def back_keep(v):
    return (v, None)

def back_low(kept, grad):
    return (low(grad),)
low.defvjp(low_keep, low_pass)
low_back.defvjp(back_keep, back_low)

def round_both(value_in):
    return low_back(low(value_in))

def matmul(left, right):
    return jnp.dot(left, right, precision=lax.Precision.HIGHEST, preferred_element_type=jnp.float32)

def norm_rows(value_in, gain, shift):
    centred = value_in - lax.optimization_barrier(jnp.mean(value_in, -1, keepdims=True))
    spread = lax.optimization_barrier(jnp.mean(centred * centred, -1, keepdims=True))
    return centred * lax.rsqrt(spread + EPSILON) * gain + shift

def one_sequence(params, seq_rows):
    w_qkv, b_qv, w_out, w_up, b_up, w_down, ln_gains, ln_shifts = params
    queries = round_both(matmul(seq_rows, w_qkv[0]) + b_qv[0].reshape(D))
    key_rows = round_both(matmul(seq_rows, w_qkv[1]))
    value_rows = round_both(matmul(seq_rows, w_qkv[2]) + b_qv[1].reshape(D))
    query_heads = queries.reshape(LEN, HEADS, HD)
    key_heads = key_rows.reshape(LEN, HEADS, HD)
    value_heads = value_rows.reshape(LEN, HEADS, HD)
    scores = low_back(jnp.einsum('qhd,khd->hqk', query_heads, key_heads, precision=lax.Precision.HIGHEST) * 0.125)
    attn_probs = low(jax.nn.softmax(scores, axis=-1))
    attended = jnp.einsum('hqk,khd->qhd', attn_probs, value_heads, precision=lax.Precision.HIGHEST)
    attended = round_both(attended.reshape(LEN, D))
    branch = low_back(matmul(attended, w_out) + ln_shifts[0])
    normed = low(norm_rows(seq_rows + branch, ln_gains[0], ln_shifts[1]))
    hidden_pre = low_back(matmul(normed, w_up) + b_up.reshape(FF))
    hidden = low(jax.nn.gelu(hidden_pre, approximate=False))
    mlp_out = low_back(matmul(hidden, w_down) + ln_shifts[2])
    return norm_rows(normed + mlp_out, ln_gains[1], ln_shifts[3])

def forward(inputs_wide, *params):
    sequences = inputs_wide.reshape(MB * SEQS, LEN, D)

    def advance(running, seq_rows):
        return (running, jax.checkpoint(one_sequence)(params, seq_rows))
    unused, results = lax.scan(advance, jnp.zeros((), jnp.float32), sequences)
    return results.reshape(MB, SEQS, LEN, D)

def reference(inputs, w_qkv, b_qv, w_out, w_up, b_up, w_down, ln_gains, ln_shifts, cotangent):
    params = tuple((p.astype(jnp.float32) for p in (w_qkv, b_qv, w_out, w_up, b_up, w_down, ln_gains, ln_shifts)))
    result, pull_back = jax.vjp(forward, inputs.astype(jnp.float32), *params)
    grads = pull_back(cotangent.astype(jnp.float32))
    return (result.astype(jnp.bfloat16), grads[0].astype(jnp.bfloat16), grads[1], grads[2], grads[3], grads[4], grads[5], grads[6], grads[7], grads[8])
```

```python
import functools

import jax
import jax.numpy as jnp
from jax import lax
from jax.experimental import pallas as pl
from jax.experimental.pallas import tpu as pltpu
from jax.sharding import PartitionSpec as P

EPSILON = 1e-05
F32 = jnp.float32
BF16 = jnp.bfloat16
MESH = pl.DeviceIdType.MESH
VMEM_SPEC = pl.BlockSpec(memory_space=pltpu.VMEM)
VMEM_LIMIT = 48 * 1024 * 1024


def dot(left, right, dims):
    return lax.dot_general(left, right, (dims, ((), ())), preferred_element_type=F32)


NN = ((1,), (0,))
NT = ((1,), (1,))
TN = ((0,), (0,))


def norm_parts(rows):
    centred = rows - jnp.mean(rows, -1, keepdims=True)
    spread = jnp.mean(centred * centred, -1, keepdims=True)
    scale = lax.rsqrt(spread + EPSILON)
    return centred * scale, scale


def norm_back(grad, unit, scale, gain):
    inner = grad * gain
    mean_one = jnp.mean(inner, -1, keepdims=True)
    mean_two = jnp.mean(inner * unit, -1, keepdims=True)
    return scale * (inner - mean_one - unit * mean_two)


def row_sum(rows):
    return jnp.sum(rows, 0, keepdims=True)


def exchange_kernel(n, parts, has_sum, has_send, tail, work, n_in, n_out, *refs):
    refs = list(refs)
    partial = refs.pop(0) if has_sum else None
    ins = [refs.pop(0) for _ in range(n_in)]
    gathered = refs.pop(0) if has_send else None
    outs = [refs.pop(0) for _ in range(n_out)]
    relay = n == 4
    if has_sum:
        landing, sum_send, sum_recv = refs.pop(0), refs.pop(0), refs.pop(0)
        if relay:
            relay_in, relay_out, relay_send, relay_recv = [refs.pop(0) for _ in range(4)]
    if has_send:
        all_send, all_recv = refs.pop(0), refs.pop(0)
    if tail:
        tail_land, tail_send, tail_recv = refs.pop(0), refs.pop(0), refs.pop(0)
    me = lax.axis_index("heads")

    def start(src, dst, send_sem, recv_sem, k):
        copy = pltpu.make_async_remote_copy(
            src_ref=src,
            dst_ref=dst,
            send_sem=send_sem,
            recv_sem=recv_sem,
            device_id={"heads": me ^ k},
            device_id_type=MESH,
        )
        copy.start()
        return copy

    barrier = pltpu.get_barrier_semaphore()
    for k in range(1, n):
        pl.semaphore_signal(barrier, inc=1, device_id={"heads": me ^ k}, device_id_type=MESH)
    pl.semaphore_wait(barrier, n - 1)

    own = (partial if has_sum else gathered).shape[2]
    halves = (pl.ds(0, own // 2), pl.ds(own // 2, own // 2))
    started = []
    sums = {}
    relays = {}
    if has_sum and relay:
        for part in range(parts):
            for k in (1, 2):
                relays[part, k] = start(
                    partial.at[part, me ^ 3, halves[k - 1]],
                    relay_in.at[part, k - 1],
                    relay_send.at[part, k - 1],
                    relay_recv.at[part, k - 1],
                    k,
                )
            for k in (1, 2):
                half = halves[k - 1]
                sums[part, k, 0] = start(
                    partial.at[part, me ^ k, half],
                    landing.at[part, k - 1, half],
                    sum_send.at[part, k - 1],
                    sum_recv.at[part, k - 1],
                    k,
                )
        for part in range(parts):
            for k in (1, 2):
                other, half = 3 - k, halves[k - 1]
                relays[part, k].wait_recv()
                relay_out[part, k - 1] = (
                    partial[part, me ^ other, half].astype(F32)
                    + relay_in[part, k - 1].astype(F32)
                ).astype(BF16)
                sums[part, other, 1] = start(
                    relay_out.at[part, k - 1],
                    landing.at[part, other - 1, half],
                    sum_send.at[part, 1 + other],
                    sum_recv.at[part, 1 + other],
                    other,
                )
    elif has_sum:
        for part in range(parts):
            for k in range(1, n):
                sums[part, k, 0] = start(
                    partial.at[part, me ^ k],
                    landing.at[part, k - 1],
                    sum_send.at[part, k - 1],
                    sum_recv.at[part, k - 1],
                    k,
                )
    neighbours = (1, 2) if relay else tuple(range(1, n))
    sends = {}
    for part in range(parts):
        total = None
        if has_sum:
            total = partial[part, me].astype(F32)
            for k in neighbours:
                sums[part, k, 0].wait_recv()
                if relay:
                    sums[part, k, 1].wait_recv()
                total = total + landing[part, k - 1].astype(F32)
        passed = work(part, total, ins, outs)
        if has_send:
            gathered[part, me] = passed
            for k in neighbours:
                sends[part, k] = start(
                    gathered.at[part, me],
                    gathered.at[part, me],
                    all_send.at[part, k - 1],
                    all_recv.at[part, k - 1],
                    k,
                )
    if tail:
        mine = [sum(ref[part] for part in range(parts)) for ref in (outs[1], ins[-1])]
        tail_land[me] = jnp.concatenate(mine + [jnp.zeros((2, mine[0].shape[1]), F32)], 0)
        tails = [
            start(tail_land.at[me], tail_land.at[me], tail_send.at[k - 1], tail_recv.at[k - 1], k)
            for k in range(1, n)
        ]
    if has_send and relay:
        for part in range(parts):
            for k in (1, 2):
                sends[part, k].wait_recv()
                half = halves[k - 1]
                other = 3 - k
                started.append(
                    start(
                        gathered.at[part, me ^ k, half],
                        gathered.at[part, me ^ k, half],
                        all_send.at[part, 1 + other],
                        all_recv.at[part, 1 + other],
                        other,
                    )
                )
        for copy in started:
            copy.wait_recv()
    elif has_send:
        for copy in sends.values():
            copy.wait_recv()
    if tail:
        for copy in tails:
            copy.wait_recv()
        outs[-1][...] = sum(tail_land[k, 0:6] for k in range(n))
        for copy in tails:
            copy.wait_send()
    for copy in list(relays.values()) + list(sums.values()) + list(sends.values()) + started:
        copy.wait_send()


def exchange(n, name, ident, work, partial, ins, out_shapes, has_send, shape, tail=False):
    parts, rows, width = shape
    has_sum = partial is not None
    relay = n == 4
    operands = ([partial] if has_sum else []) + list(ins)
    shapes = ([jax.ShapeDtypeStruct((parts, n, rows, width), BF16)] if has_send else []) + [
        jax.ShapeDtypeStruct(s, t) for s, t in out_shapes
    ]
    sems = pltpu.SemaphoreType.DMA((parts, 4 if relay else n - 1))
    scratch = []
    if has_sum:
        scratch += [pltpu.VMEM((parts, 2 if relay else n - 1, rows, width), BF16), sems, sems]
        if relay:
            scratch += [pltpu.VMEM((parts, 2, rows // 2, width), BF16)] * 2
            scratch += [pltpu.SemaphoreType.DMA((parts, 2))] * 2
    if has_send:
        scratch += [sems, sems]
    if tail:
        scratch += [pltpu.VMEM((n, 8, width), F32)] + [pltpu.SemaphoreType.DMA((n - 1,))] * 2
    return pl.pallas_call(
        functools.partial(
            exchange_kernel, n, parts, has_sum, has_send, tail, work, len(ins), len(out_shapes)
        ),
        out_shape=shapes,
        in_specs=[VMEM_SPEC] * len(operands),
        out_specs=[VMEM_SPEC] * len(shapes),
        scratch_shapes=scratch,
        compiler_params=pltpu.CompilerParams(
            collective_id=ident, has_side_effects=True, vmem_limit_bytes=VMEM_LIMIT
        ),
        cost_estimate=pl.CostEstimate(
            flops=1000000, bytes_accessed=60000000, transcendentals=0
        ),
        name=name,
    )(*operands)


def work_inputs(part, total, ins, outs):
    return ins[0][part]


def work_first(part, total, ins, outs):
    x_rows, gains, shifts = ins
    first = x_rows[part].astype(F32) + total + shifts[0:1]
    outs[0][part] = first
    unit, _ = norm_parts(first)
    normed = (unit * gains[0:1] + shifts[1:2]).astype(BF16)
    outs[1][part] = normed
    return normed


def work_second(part, total, ins, outs):
    normed, cotangent, gains, shifts = ins
    second = normed[part].astype(F32) + total + shifts[2:3]
    unit, scale = norm_parts(second)
    outs[0][part] = (unit * gains[1:2] + shifts[3:4]).astype(BF16)
    grad = cotangent[part].astype(F32)
    d_second = norm_back(grad, unit, scale, gains[1:2])
    outs[1][part] = d_second
    low = d_second.astype(BF16)
    sums = jnp.concatenate(
        [row_sum(grad * unit), row_sum(low.astype(F32)), row_sum(grad)], 0
    )
    outs[2][part] = sums
    return low


def work_third(part, total, ins, outs):
    first, d_second, gains, _ = ins
    grad = total + d_second[part]
    unit, scale = norm_parts(first[part])
    d_first = norm_back(grad, unit, scale, gains[0:1])
    outs[0][part] = d_first
    low = d_first.astype(BF16)
    sums = jnp.concatenate(
        [row_sum(grad * unit), row_sum(low.astype(F32)), row_sum(grad)], 0
    )
    outs[1][part] = sums
    return low


def work_last(part, total, ins, outs):
    outs[0][part] = (total + ins[0][part]).astype(BF16)
    return None


def attend_kernel(head, q_ref, k_ref, v_ref, k_far, v_far, o_ref, log_ref):
    queries = q_ref[0] * jnp.asarray(0.125, BF16)
    keys = jnp.concatenate([k_ref[0], k_far[0]], 0)
    values = jnp.concatenate([v_ref[0], v_far[0]], 0)
    mixed, logs = [], []
    for h in range(q_ref.shape[-1] // head):
        cols = slice(h * head, (h + 1) * head)
        scores = dot(keys[:, cols], queries[:, cols], NT)
        largest = jnp.max(scores, 0, keepdims=True)
        weights = jnp.exp(scores - largest)
        totals = jnp.sum(weights, 0, keepdims=True)
        probs = (weights * (1.0 / totals)).astype(BF16)
        mixed.append(dot(probs, values[:, cols], TN))
        logs.append(largest + jnp.log(totals))
    o_ref[0] = jnp.concatenate(mixed, -1).astype(BF16)
    log_ref[0, 0] = jnp.concatenate(logs, 0)


def attend_back_kernel(
    head, q_ref, k_ref, v_ref, k_far, v_far, do_ref, log_ref, dq_ref, dkv_ref, far_ref
):
    half = k_ref.shape[1]
    queries = q_ref[0] * jnp.asarray(0.125, BF16)
    keys = jnp.concatenate([k_ref[0], k_far[0]], 0)
    values = jnp.concatenate([v_ref[0], v_far[0]], 0)
    d_mixed = do_ref[0]
    dq, dk, dv = [], [], []
    for h in range(q_ref.shape[-1] // head):
        cols = slice(h * head, (h + 1) * head)
        scores = dot(keys[:, cols], queries[:, cols], NT)
        probs = jnp.exp(scores - log_ref[0, 0, h : h + 1])
        d_probs = dot(values[:, cols], d_mixed[:, cols], NT)
        centre = jnp.sum(probs * d_probs, 0, keepdims=True)
        d_scores = (probs * (d_probs - centre)).astype(BF16)
        dv.append(dot(probs.astype(BF16), d_mixed[:, cols], NN))
        dk.append(dot(d_scores, queries[:, cols], NN))
        dq.append(dot(d_scores, keys[:, cols], TN) * 0.125)
    dq_ref[0] = jnp.concatenate(dq, -1).astype(BF16)
    for at, rows in enumerate((dk, dv)):
        rows = jnp.concatenate(rows, -1)
        dkv_ref[at, 0] = rows[:half]
        far_ref[at, 0] = rows[half:].astype(BF16)


def attention_call(kernel, name, queries, kv, kv_far, more, more_logs, outs, dots, head):
    micro, rows, width = queries.shape
    half = kv.shape[1]
    block = min(128, width)
    blocks = width // block
    row_spec = pl.BlockSpec((1, rows, block), lambda m, j: (m, 0, j))
    log_spec = pl.BlockSpec((1, 1, block // head, rows), lambda m, j: (m, j, 0, 0))
    pair_spec = pl.BlockSpec((2, 1, half, block), lambda m, j: (0, m, 0, j))
    shared = block % 128 == 0
    skip = blocks if shared else 0
    value_spec = pl.BlockSpec((1, half, block), lambda m, j: (m, 0, j + skip))
    both = [(v, v) if shared else (v[..., :width], v[..., width:]) for v in (kv, kv_far)]
    kinds = {
        "row": (row_spec, jax.ShapeDtypeStruct(queries.shape, BF16)),
        "log": (log_spec, jax.ShapeDtypeStruct((micro, blocks, block // head, rows), F32)),
        "pair": (pair_spec, jax.ShapeDtypeStruct((2, micro, half, width), F32)),
        "far": (pair_spec, jax.ShapeDtypeStruct((2, micro, half, width), BF16)),
    }
    return pl.pallas_call(
        functools.partial(kernel, head),
        grid=(micro, blocks),
        in_specs=[row_spec] + [row_spec, value_spec] * 2
        + [row_spec] * len(more) + [log_spec] * len(more_logs),
        out_specs=[kinds[k][0] for k in outs],
        out_shape=[kinds[k][1] for k in outs],
        compiler_params=pltpu.CompilerParams(vmem_limit_bytes=VMEM_LIMIT),
        cost_estimate=pl.CostEstimate(
            flops=2 * dots * micro * rows * 2 * half * width * 4,
            bytes_accessed=20000000,
            transcendentals=0,
        ),
        name=name,
    )(queries, *both[0], *both[1], *more, *more_logs)


def gelu_parts(value):
    cdf = 0.5 * (1.0 + lax.erf(value * 0.7071067811865476))
    return cdf, 0.3989422804014327 * jnp.exp(-0.5 * value * value)


def local(inputs, w_qkv, b_qv, w_out, w_up, b_up, w_down, ln_gains, ln_shifts, cotangent):
    n = lax.axis_size("heads")
    owners = lax.axis_size("dp") * lax.axis_size("seq")
    share = ("dp", "seq")
    micro, _, own, width = inputs.shape
    rows = n * own
    heads_here, head = b_qv.shape[1], b_qv.shape[2] * owners
    cols = heads_here * head
    depth = w_qkv.shape[1]
    hidden_here = w_up.shape[1]
    piece = (micro, own, width)

    small = jnp.concatenate([v.reshape(-1) for v in (b_qv, b_up, ln_gains, ln_shifts)])
    small_rows = -(-small.size // (3 * cols * 16)) * 16
    small = jnp.pad(small, (0, small_rows * 3 * cols - small.size)).reshape(small_rows, 3 * cols)
    qkv_mine = jnp.concatenate([jnp.swapaxes(w_qkv, 0, 1).reshape(depth, 3 * cols), small], 0)
    qkv_all = lax.all_gather(qkv_mine, share, axis=0, tiled=False)
    x_rows = inputs[:, 0]
    (gathered,) = exchange(n, "gather_inputs", 0, work_inputs, None, [x_rows], [], True, piece)
    gathered = gathered.reshape(micro * rows, width)
    out_all = lax.all_gather(w_out.T, share, axis=0, tiled=True)
    up_all = lax.all_gather(w_up, share, axis=0, tiled=True)
    down_all = lax.all_gather(w_down.T, share, axis=0, tiled=True)

    q_weights = qkv_all[:, :depth, :cols].reshape(owners * depth, cols)
    kv_weights = qkv_all[:, :depth, cols:].reshape(owners * depth, 2 * cols)
    small_all = qkv_all[:, depth:].reshape(owners, -1)
    at = 0
    pieces = []
    for v in (b_qv, b_up, ln_gains, ln_shifts):
        part = small_all[:, at : at + v.size].reshape((owners,) + v.shape)
        pieces.append(jnp.moveaxis(part, 0, -2).reshape(v.shape[:-1] + (-1,)).astype(F32))
        at += v.size
    bias_qv, bias_up, gains, shifts = pieces
    bias_qv = bias_qv.reshape(2, cols)
    bias_kv = jnp.concatenate([jnp.zeros_like(bias_qv[0]), bias_qv[1]])
    swap = [(0, 1), (1, 0)]

    kv = (dot(gathered, kv_weights, NN) + bias_kv).astype(BF16).reshape(micro, rows, 2 * cols)
    kv_far = lax.ppermute(kv, "seq", swap)
    queries = (dot(gathered, q_weights, NN) + bias_qv[0]).astype(BF16).reshape(micro, rows, cols)
    mixed, logs = attention_call(
        attend_kernel, "attend", queries, kv, kv_far, [], [], ["row", "log"], 2, head
    )
    mixed_rows = mixed.reshape(micro * rows, cols)
    partial = dot(mixed_rows, out_all, NT).astype(BF16).reshape(micro, n, own, width)
    normed_all, first, normed = exchange(
        n, "first_norm", 1, work_first, partial, [x_rows, gains, shifts],
        [(piece, F32), (piece, BF16)], True, piece,
    )
    normed_all = normed_all.reshape(micro * rows, width)
    hidden_pre = dot(normed_all, up_all, NN) + bias_up.reshape(-1)
    cdf, density = gelu_parts(hidden_pre)
    hidden = (hidden_pre * cdf).astype(BF16)
    slope = cdf + hidden_pre * density
    partial = dot(hidden, down_all, NT).astype(BF16).reshape(micro, n, own, width)
    d_mlp, result, d_second, sums_two = exchange(
        n, "second_norm", 2, work_second, partial, [normed, cotangent[:, 0], gains, shifts],
        [(piece, BF16), (piece, F32), ((micro, 3, width), F32)], True, piece,
    )

    d_mlp = d_mlp.reshape(micro * rows, width)
    d_pre_wide = dot(d_mlp, down_all, NN) * slope
    d_pre = d_pre_wide.astype(BF16)
    partial = dot(d_pre, up_all, NT).astype(BF16).reshape(micro, n, own, width)
    g_down = dot(d_mlp, hidden, TN).astype(BF16)
    g_up = dot(normed_all, d_pre, TN).astype(BF16)
    g_bup = jnp.sum(d_pre.astype(F32), 0).reshape(b_up.shape[0], owners, b_up.shape[1])
    g_bup = jnp.swapaxes(g_bup, 0, 1).reshape(owners, -1)

    def with_extra(wide, extra):
        wide = wide.reshape(owners, -1, wide.shape[-1])
        span = wide.shape[-1]
        extra = jnp.pad(extra, ((0, 0), (0, -extra.shape[-1] % (16 * span)))).astype(BF16)
        return jnp.concatenate([wide, extra.reshape(owners, -1, span)], 1)

    g_up = with_extra(g_up, g_bup)
    partial, g_down, g_up = lax.optimization_barrier((partial, g_down, g_up))
    g_down = lax.psum_scatter(g_down, share, scatter_dimension=0, tiled=True)
    g_up = lax.psum_scatter(g_up, share, scatter_dimension=0, tiled=False)
    d_attn, d_first, _, norm_sums = exchange(
        n, "first_norm_back", 3, work_third, partial, [first, d_second, gains, sums_two],
        [(piece, F32), ((micro, 3, width), F32), ((6, width), F32)], True, piece, tail=True,
    )

    d_attn = d_attn.reshape(micro * rows, width)
    d_mixed = dot(d_attn, out_all, NN).astype(BF16).reshape(micro, rows, cols)
    norm_sums = jnp.swapaxes(norm_sums.reshape(6, owners, depth), 0, 1).reshape(owners, -1)
    g_out = with_extra(dot(d_attn, mixed_rows, TN).astype(BF16), norm_sums)
    d_mixed, g_out = lax.optimization_barrier((d_mixed, g_out))
    g_out = lax.psum_scatter(g_out, share, scatter_dimension=0, tiled=False)
    d_query, d_kv, d_far = attention_call(
        attend_back_kernel, "attend_back", queries, kv, kv_far, [d_mixed], [logs],
        ["row", "pair", "far"], 5, head,
    )
    d_kv = (d_kv + lax.ppermute(d_far, "seq", swap).astype(F32)).astype(BF16)
    d_qkv = jnp.concatenate([d_query, d_kv[0], d_kv[1]], -1).reshape(micro * rows, 3 * cols)
    qkv_weights = qkv_all[:, :depth].reshape(owners * depth, 3 * cols)
    partial = dot(d_qkv, qkv_weights, NT).astype(BF16).reshape(micro, n, own, width)
    sums = jnp.sum(d_qkv.astype(F32), 0).reshape(3, heads_here, owners, head // owners)
    g_bqv = jnp.moveaxis(jnp.stack([sums[0], sums[2]]), 2, 0).reshape(owners, -1)
    g_qkv = with_extra(dot(gathered, d_qkv, TN).astype(BF16), g_bqv)
    partial, g_qkv = lax.optimization_barrier((partial, g_qkv))
    g_qkv = lax.psum_scatter(g_qkv, share, scatter_dimension=0, tiled=False)
    (d_inputs,) = exchange(
        n, "input_grad", 4, work_last, partial, [d_first], [(piece, BF16)], False, piece
    )

    norm_mine = g_out[depth:].reshape(-1)[: 6 * depth].astype(F32).reshape(6, depth)
    gain_grad = jnp.stack([norm_mine[0], norm_mine[3]])
    shift_grad = jnp.stack([norm_mine[1], norm_mine[2], norm_mine[4], norm_mine[5]])
    qkv_grad = jnp.swapaxes(g_qkv[:depth].astype(F32).reshape(depth, 3, cols), 0, 1)
    bqv_grad = g_qkv[depth:].reshape(-1)[: b_qv.size].astype(F32).reshape(b_qv.shape)
    up_grad = g_up[:depth].astype(F32)
    bup_grad = g_up[depth:].reshape(-1)[: b_up.size].astype(F32).reshape(b_up.shape)
    return (
        result[:, None],
        d_inputs[:, None],
        qkv_grad,
        bqv_grad,
        g_out[:depth].astype(F32).T,
        up_grad,
        bup_grad,
        g_down.astype(F32).T,
        gain_grad,
        shift_grad,
    )


def solution(mesh):
    rows_spec = P(None, "dp", ("seq", "heads"), None)
    weight_specs = (
        P(None, ("dp", "seq"), "heads"),
        P(None, "heads", ("dp", "seq")),
        P("heads", ("dp", "seq")),
        P(("dp", "seq"), "heads"),
        P("heads", ("dp", "seq")),
        P("heads", ("dp", "seq")),
        P(None, ("dp", "seq")),
        P(None, ("dp", "seq")),
    )
    return jax.shard_map(
        local,
        mesh=mesh,
        in_specs=(rows_spec,) + weight_specs + (rows_spec,),
        out_specs=(rows_spec, rows_spec) + weight_specs,
        check_vma=False,
    )
```

```python
import functools

import jax
import jax.numpy as jnp
from jax import lax
from jax.experimental import pallas as pl
from jax.experimental.pallas import tpu as pltpu
from jax.sharding import PartitionSpec as P

EPSILON = 1e-05
F32 = jnp.float32
BF16 = jnp.bfloat16
MESH = pl.DeviceIdType.MESH
VMEM_SPEC = pl.BlockSpec(memory_space=pltpu.VMEM)
VMEM_LIMIT = 48 * 1024 * 1024


def dot(left, right, dims):
    return lax.dot_general(left, right, (dims, ((), ())), preferred_element_type=F32)


NN = ((1,), (0,))
NT = ((1,), (1,))
TN = ((0,), (0,))


def norm_parts(rows):
    centred = rows - jnp.mean(rows, -1, keepdims=True)
    spread = jnp.mean(centred * centred, -1, keepdims=True)
    scale = lax.rsqrt(spread + EPSILON)
    return centred * scale, scale


def norm_back(grad, unit, scale, gain):
    inner = grad * gain
    mean_one = jnp.mean(inner, -1, keepdims=True)
    mean_two = jnp.mean(inner * unit, -1, keepdims=True)
    return scale * (inner - mean_one - unit * mean_two)


def row_sum(rows):
    return jnp.sum(rows, 0, keepdims=True)


def exchange_kernel(n, far, parts, has_sum, has_send, tail, work, n_in, n_out, n_grad, *refs):
    refs = list(refs)
    partial = refs.pop(0) if has_sum else None
    ins = [refs.pop(0) for _ in range(n_in)]
    grads = [refs.pop(0) for _ in range(n_grad)]
    gathered = refs.pop(0) if has_send else None
    outs = [refs.pop(0) for _ in range(n_out)]
    grad_outs = [refs.pop(0) for _ in range(n_grad)]
    relay = n == 4
    if has_sum:
        landing, sum_send, sum_recv = refs.pop(0), refs.pop(0), refs.pop(0)
        if relay:
            relay_in, relay_out, relay_send, relay_recv = [refs.pop(0) for _ in range(4)]
    if has_send:
        all_send, all_recv = refs.pop(0), refs.pop(0)
    if tail:
        tail_land, tail_send, tail_recv = refs.pop(0), refs.pop(0), refs.pop(0)
    grad_scratch = [[refs.pop(0) for _ in range(6)] for _ in range(n_grad)]
    me = lax.axis_index("heads")

    def start_at(src, dst, send_sem, recv_sem, target):
        copy = pltpu.make_async_remote_copy(
            src_ref=src,
            dst_ref=dst,
            send_sem=send_sem,
            recv_sem=recv_sem,
            device_id=target,
            device_id_type=MESH,
        )
        copy.start()
        return copy

    def start(src, dst, send_sem, recv_sem, k):
        return start_at(src, dst, send_sem, recv_sem, {"heads": me ^ k})

    barrier = pltpu.get_barrier_semaphore()
    for k in range(1, n):
        pl.semaphore_signal(barrier, inc=1, device_id={"heads": me ^ k}, device_id_type=MESH)
    if n_grad:
        side = lax.axis_index("seq")
        place = lax.axis_index("dp")
        ahead = [lax.rem(place + j, far) for j in range(far)]
        for target in [{"seq": 1 - side}] + [{"dp": ahead[j]} for j in range(1, far)]:
            pl.semaphore_signal(barrier, inc=1, device_id=target, device_id_type=MESH)
    pl.semaphore_wait(barrier, n - 1 + (far if n_grad else 0))

    core_copies, far_copies = {}, {}
    for at, (ref, scratch) in enumerate(zip(grads, grad_scratch)):
        for j in list(range(1, far)) + [0]:
            core_copies[at, j] = start_at(
                ref.at[2 * ahead[j] + 1 - side],
                scratch[0].at[ahead[j]],
                scratch[2].at[j],
                scratch[3].at[j],
                {"seq": 1 - side},
            )

    own = (partial if has_sum else gathered).shape[2]
    halves = (pl.ds(0, own // 2), pl.ds(own // 2, own // 2))
    started = []
    sums = {}
    relays = {}
    if has_sum and relay:
        for part in range(parts):
            for k in (1, 2):
                relays[part, k] = start(
                    partial.at[part, me ^ 3, halves[k - 1]],
                    relay_in.at[part, k - 1],
                    relay_send.at[part, k - 1],
                    relay_recv.at[part, k - 1],
                    k,
                )
            for k in (1, 2):
                half = halves[k - 1]
                sums[part, k, 0] = start(
                    partial.at[part, me ^ k, half],
                    landing.at[part, k - 1, half],
                    sum_send.at[part, k - 1],
                    sum_recv.at[part, k - 1],
                    k,
                )
    for at, (ref, scratch) in enumerate(zip(grads, grad_scratch)):
        for j in range(1, far):
            core_copies[at, j].wait_recv()
            scratch[0][ahead[j]] = (
                ref[2 * ahead[j] + side].astype(F32) + scratch[0][ahead[j]].astype(F32)
            ).astype(ref.dtype)
            far_copies[at, j] = start_at(
                scratch[0].at[ahead[j]],
                scratch[1].at[j - 1],
                scratch[4].at[j - 1],
                scratch[5].at[j - 1],
                {"dp": ahead[j]},
            )
    if has_sum and relay:
        for part in range(parts):
            for k in (1, 2):
                other, half = 3 - k, halves[k - 1]
                relays[part, k].wait_recv()
                relay_out[part, k - 1] = (
                    partial[part, me ^ other, half].astype(F32)
                    + relay_in[part, k - 1].astype(F32)
                ).astype(BF16)
                sums[part, other, 1] = start(
                    relay_out.at[part, k - 1],
                    landing.at[part, other - 1, half],
                    sum_send.at[part, 1 + other],
                    sum_recv.at[part, 1 + other],
                    other,
                )
    if has_sum and not relay:
        for part in range(parts):
            for k in range(1, n):
                sums[part, k, 0] = start(
                    partial.at[part, me ^ k],
                    landing.at[part, k - 1],
                    sum_send.at[part, k - 1],
                    sum_recv.at[part, k - 1],
                    k,
                )
    neighbours = (1, 2) if relay else tuple(range(1, n))
    sends = {}
    for part in range(parts):
        total = None
        if has_sum:
            total = partial[part, me].astype(F32)
            for k in neighbours:
                sums[part, k, 0].wait_recv()
                if relay:
                    sums[part, k, 1].wait_recv()
                total = total + landing[part, k - 1].astype(F32)
        passed = work(part, total, ins, outs)
        if has_send:
            gathered[part, me] = passed
            for k in neighbours:
                sends[part, k] = start(
                    gathered.at[part, me],
                    gathered.at[part, me],
                    all_send.at[part, k - 1],
                    all_recv.at[part, k - 1],
                    k,
                )
    if tail:
        mine = [sum(ref[part] for part in range(parts)) for ref in (outs[1], ins[-1])]
        tail_land[me] = jnp.concatenate(mine + [jnp.zeros((2, mine[0].shape[1]), F32)], 0)
        tails = [
            start(tail_land.at[me], tail_land.at[me], tail_send.at[k - 1], tail_recv.at[k - 1], k)
            for k in range(1, n)
        ]
    if has_send and relay:
        for part in range(parts):
            for k in (1, 2):
                sends[part, k].wait_recv()
                half = halves[k - 1]
                other = 3 - k
                started.append(
                    start(
                        gathered.at[part, me ^ k, half],
                        gathered.at[part, me ^ k, half],
                        all_send.at[part, 1 + other],
                        all_recv.at[part, 1 + other],
                        other,
                    )
                )
        for copy in started:
            copy.wait_recv()
    elif has_send:
        for copy in sends.values():
            copy.wait_recv()
    if tail:
        for copy in tails:
            copy.wait_recv()
        outs[-1][...] = sum(tail_land[k, 0:6] for k in range(n))
        for copy in tails:
            copy.wait_send()
    for at, (ref, scratch) in enumerate(zip(grads, grad_scratch)):
        core_copies[at, 0].wait_recv()
        total = ref[2 * place + side].astype(F32) + scratch[0][place].astype(F32)
        for j in range(1, far):
            far_copies[at, j].wait_recv()
            total = total + scratch[1][j - 1].astype(F32)
        grad_outs[at][...] = total
    started += list(core_copies.values()) + list(far_copies.values())
    for copy in list(relays.values()) + list(sums.values()) + list(sends.values()) + started:
        copy.wait_send()


def exchange(n, name, ident, work, partial, ins, out_shapes, has_send, shape, tail=False, grads=()):
    parts, rows, width = shape
    has_sum = partial is not None
    relay = n == 4
    far = lax.axis_size("dp")
    operands = ([partial] if has_sum else []) + list(ins) + list(grads)
    shapes = ([jax.ShapeDtypeStruct((parts, n, rows, width), BF16)] if has_send else []) + [
        jax.ShapeDtypeStruct(s, t) for s, t in out_shapes
    ]
    shapes += [jax.ShapeDtypeStruct(g.shape[1:], F32) for g in grads]
    sems = pltpu.SemaphoreType.DMA((parts, 4 if relay else n - 1))
    scratch = []
    if has_sum:
        scratch += [pltpu.VMEM((parts, 2 if relay else n - 1, rows, width), BF16), sems, sems]
        if relay:
            scratch += [pltpu.VMEM((parts, 2, rows // 2, width), BF16)] * 2
            scratch += [pltpu.SemaphoreType.DMA((parts, 2))] * 2
    if has_send:
        scratch += [sems, sems]
    if tail:
        scratch += [pltpu.VMEM((n, 8, width), F32)] + [pltpu.SemaphoreType.DMA((n - 1,))] * 2
    for g in grads:
        scratch += [pltpu.VMEM((count,) + g.shape[1:], g.dtype) for count in (far, far - 1)]
        scratch += [pltpu.SemaphoreType.DMA((far,))] * 2 + [pltpu.SemaphoreType.DMA((far - 1,))] * 2
    return pl.pallas_call(
        functools.partial(
            exchange_kernel, n, far, parts, has_sum, has_send, tail, work, len(ins),
            len(out_shapes), len(grads),
        ),
        out_shape=shapes,
        in_specs=[VMEM_SPEC] * len(operands),
        out_specs=[VMEM_SPEC] * len(shapes),
        scratch_shapes=scratch,
        compiler_params=pltpu.CompilerParams(
            collective_id=ident, has_side_effects=True, vmem_limit_bytes=VMEM_LIMIT
        ),
        cost_estimate=pl.CostEstimate(
            flops=1000000, bytes_accessed=60000000, transcendentals=0
        ),
        name=name,
    )(*operands)


def work_inputs(part, total, ins, outs):
    return ins[0][part]


def work_first(part, total, ins, outs):
    x_rows, gains, shifts = ins
    first = x_rows[part].astype(F32) + total + shifts[0:1]
    outs[0][part] = first
    unit, _ = norm_parts(first)
    normed = (unit * gains[0:1] + shifts[1:2]).astype(BF16)
    outs[1][part] = normed
    return normed


def work_second(part, total, ins, outs):
    normed, cotangent, gains, shifts = ins
    second = normed[part].astype(F32) + total + shifts[2:3]
    unit, scale = norm_parts(second)
    outs[0][part] = (unit * gains[1:2] + shifts[3:4]).astype(BF16)
    grad = cotangent[part].astype(F32)
    d_second = norm_back(grad, unit, scale, gains[1:2])
    outs[1][part] = d_second
    low = d_second.astype(BF16)
    sums = jnp.concatenate(
        [row_sum(grad * unit), row_sum(low.astype(F32)), row_sum(grad)], 0
    )
    outs[2][part] = sums
    return low


def work_third(part, total, ins, outs):
    first, d_second, gains, _ = ins
    grad = total + d_second[part]
    unit, scale = norm_parts(first[part])
    d_first = norm_back(grad, unit, scale, gains[0:1])
    outs[0][part] = d_first
    low = d_first.astype(BF16)
    sums = jnp.concatenate(
        [row_sum(grad * unit), row_sum(low.astype(F32)), row_sum(grad)], 0
    )
    outs[1][part] = sums
    return low


def work_last(part, total, ins, outs):
    outs[0][part] = (total + ins[0][part]).astype(BF16)
    return None


def attend_kernel(head, q_ref, k_ref, v_ref, k_far, v_far, o_ref, log_ref):
    queries = q_ref[0] * jnp.asarray(0.125, BF16)
    keys = jnp.concatenate([k_ref[0], k_far[0]], 0)
    values = jnp.concatenate([v_ref[0], v_far[0]], 0)
    mixed, logs = [], []
    for h in range(q_ref.shape[-1] // head):
        cols = slice(h * head, (h + 1) * head)
        scores = dot(keys[:, cols], queries[:, cols], NT)
        largest = jnp.max(scores, 0, keepdims=True)
        weights = jnp.exp(scores - largest)
        totals = jnp.sum(weights, 0, keepdims=True)
        probs = (weights * (1.0 / totals)).astype(BF16)
        mixed.append(dot(probs, values[:, cols], TN))
        logs.append(largest + jnp.log(totals))
    o_ref[0] = jnp.concatenate(mixed, -1).astype(BF16)
    log_ref[0, 0] = jnp.concatenate(logs, 0)


def attend_back_kernel(
    head, q_ref, k_ref, v_ref, k_far, v_far, do_ref, log_ref, dq_ref, dkv_ref, far_ref
):
    half = k_ref.shape[1]
    queries = q_ref[0] * jnp.asarray(0.125, BF16)
    keys = jnp.concatenate([k_ref[0], k_far[0]], 0)
    values = jnp.concatenate([v_ref[0], v_far[0]], 0)
    d_mixed = do_ref[0]
    dq, dk, dv = [], [], []
    for h in range(q_ref.shape[-1] // head):
        cols = slice(h * head, (h + 1) * head)
        scores = dot(keys[:, cols], queries[:, cols], NT)
        probs = jnp.exp(scores - log_ref[0, 0, h : h + 1])
        d_probs = dot(values[:, cols], d_mixed[:, cols], NT)
        centre = jnp.sum(probs * d_probs, 0, keepdims=True)
        d_scores = (probs * (d_probs - centre)).astype(BF16)
        dv.append(dot(probs.astype(BF16), d_mixed[:, cols], NN))
        dk.append(dot(d_scores, queries[:, cols], NN))
        dq.append(dot(d_scores, keys[:, cols], TN) * 0.125)
    dq_ref[0] = jnp.concatenate(dq, -1).astype(BF16)
    for at, rows in enumerate((dk, dv)):
        rows = jnp.concatenate(rows, -1)
        dkv_ref[at, 0] = rows[:half]
        far_ref[at, 0] = rows[half:].astype(BF16)


def attention_call(kernel, name, queries, kv, kv_far, more, more_logs, outs, dots, head):
    micro, rows, width = queries.shape
    half = kv.shape[1]
    block = min(128, width)
    blocks = width // block
    row_spec = pl.BlockSpec((1, rows, block), lambda m, j: (m, 0, j))
    log_spec = pl.BlockSpec((1, 1, block // head, rows), lambda m, j: (m, j, 0, 0))
    pair_spec = pl.BlockSpec((2, 1, half, block), lambda m, j: (0, m, 0, j))
    shared = block % 128 == 0
    skip = blocks if shared else 0
    value_spec = pl.BlockSpec((1, half, block), lambda m, j: (m, 0, j + skip))
    both = [(v, v) if shared else (v[..., :width], v[..., width:]) for v in (kv, kv_far)]
    kinds = {
        "row": (row_spec, jax.ShapeDtypeStruct(queries.shape, BF16)),
        "log": (log_spec, jax.ShapeDtypeStruct((micro, blocks, block // head, rows), F32)),
        "pair": (pair_spec, jax.ShapeDtypeStruct((2, micro, half, width), F32)),
        "far": (pair_spec, jax.ShapeDtypeStruct((2, micro, half, width), BF16)),
    }
    return pl.pallas_call(
        functools.partial(kernel, head),
        grid=(micro, blocks),
        in_specs=[row_spec] + [row_spec, value_spec] * 2
        + [row_spec] * len(more) + [log_spec] * len(more_logs),
        out_specs=[kinds[k][0] for k in outs],
        out_shape=[kinds[k][1] for k in outs],
        compiler_params=pltpu.CompilerParams(vmem_limit_bytes=VMEM_LIMIT),
        cost_estimate=pl.CostEstimate(
            flops=2 * dots * micro * rows * 2 * half * width * 4,
            bytes_accessed=20000000,
            transcendentals=0,
        ),
        name=name,
    )(queries, *both[0], *both[1], *more, *more_logs)


def gelu_parts(value):
    cdf = 0.5 * (1.0 + lax.erf(value * 0.7071067811865476))
    return cdf, 0.3989422804014327 * jnp.exp(-0.5 * value * value)


def local(inputs, w_qkv, b_qv, w_out, w_up, b_up, w_down, ln_gains, ln_shifts, cotangent):
    n = lax.axis_size("heads")
    owners = lax.axis_size("dp") * lax.axis_size("seq")
    share = ("dp", "seq")
    micro, _, own, width = inputs.shape
    rows = n * own
    heads_here, head = b_qv.shape[1], b_qv.shape[2] * owners
    cols = heads_here * head
    depth = w_qkv.shape[1]
    hidden_here = w_up.shape[1]
    piece = (micro, own, width)

    small = jnp.concatenate([v.reshape(-1) for v in (b_qv, b_up, ln_gains, ln_shifts)])
    small = jnp.pad(small, (0, -small.size % (16 * 4 * cols))).reshape(-1, 4 * cols)
    attn_mine = jnp.concatenate([w_qkv[0], w_qkv[1], w_qkv[2], w_out.T], 1)
    attn_all = lax.all_gather(jnp.concatenate([attn_mine, small], 0), share, axis=0, tiled=False)
    x_rows = inputs[:, 0]
    (gathered,) = exchange(n, "gather_inputs", 0, work_inputs, None, [x_rows], [], True, piece)
    gathered = gathered.reshape(micro * rows, width)
    up_all = lax.all_gather(w_up, share, axis=0, tiled=True)
    down_all = lax.all_gather(w_down.T, share, axis=0, tiled=True)

    attn_weights = attn_all[:, :depth].reshape(owners * depth, 4 * cols)
    q_weights = attn_weights[:, :cols]
    kv_weights = attn_weights[:, cols : 3 * cols]
    qkv_weights = attn_weights[:, : 3 * cols]
    out_all = attn_weights[:, 3 * cols :]
    small_all = attn_all[:, depth:].reshape(owners, -1)
    at = 0
    pieces = []
    for v in (b_qv, b_up, ln_gains, ln_shifts):
        part = small_all[:, at : at + v.size].reshape((owners,) + v.shape)
        pieces.append(jnp.moveaxis(part, 0, -2).reshape(v.shape[:-1] + (-1,)).astype(F32))
        at += v.size
    bias_qv, bias_up, gains, shifts = pieces
    bias_qv = bias_qv.reshape(2, cols)
    bias_kv = jnp.concatenate([jnp.zeros_like(bias_qv[0]), bias_qv[1]])
    swap = [(0, 1), (1, 0)]

    kv = (dot(gathered, kv_weights, NN) + bias_kv).astype(BF16).reshape(micro, rows, 2 * cols)
    kv_far = lax.ppermute(kv, "seq", swap)
    queries = (dot(gathered, q_weights, NN) + bias_qv[0]).astype(BF16).reshape(micro, rows, cols)
    mixed, logs = attention_call(
        attend_kernel, "attend", queries, kv, kv_far, [], [], ["row", "log"], 2, head
    )
    mixed_rows = mixed.reshape(micro * rows, cols)
    partial = dot(mixed_rows, out_all, NT).astype(BF16).reshape(micro, n, own, width)
    normed_all, first, normed = exchange(
        n, "first_norm", 1, work_first, partial, [x_rows, gains, shifts],
        [(piece, F32), (piece, BF16)], True, piece,
    )
    normed_all = normed_all.reshape(micro * rows, width)
    hidden_pre = dot(normed_all, up_all, NN) + bias_up.reshape(-1)
    cdf, density = gelu_parts(hidden_pre)
    hidden = (hidden_pre * cdf).astype(BF16)
    slope = cdf + hidden_pre * density
    partial = dot(hidden, down_all, NT).astype(BF16).reshape(micro, n, own, width)
    d_mlp, result, d_second, sums_two = exchange(
        n, "second_norm", 2, work_second, partial, [normed, cotangent[:, 0], gains, shifts],
        [(piece, BF16), (piece, F32), ((micro, 3, width), F32)], True, piece,
    )

    d_mlp = d_mlp.reshape(micro * rows, width)
    d_pre_wide = dot(d_mlp, down_all, NN) * slope
    d_pre = d_pre_wide.astype(BF16)
    partial = dot(d_pre, up_all, NT).astype(BF16).reshape(micro, n, own, width)
    def owned(wide):
        return wide.astype(BF16).reshape(owners, -1, wide.shape[-1])

    def owned_small(values):
        return jnp.pad(values, ((0, 0), (0, -values.shape[-1] % 1024))).reshape(owners, 8, -1)

    g_down = owned(dot(d_mlp, hidden, TN))
    g_up = owned(dot(normed_all, d_pre, TN))
    g_bup = jnp.sum(d_pre.astype(F32), 0).reshape(b_up.shape[0], owners, b_up.shape[1])
    g_bup = owned_small(jnp.swapaxes(g_bup, 0, 1).reshape(owners, -1))
    d_attn, d_first, _, norm_sums, g_down, g_up, g_bup = exchange(
        n, "first_norm_back", 3, work_third, partial, [first, d_second, gains, sums_two],
        [(piece, F32), ((micro, 3, width), F32), ((6, width), F32)], True, piece, tail=True,
        grads=[g_down, g_up, g_bup],
    )

    d_attn = d_attn.reshape(micro * rows, width)
    d_mixed = dot(d_attn, out_all, NN).astype(BF16).reshape(micro, rows, cols)
    norm_sums = jnp.swapaxes(norm_sums.reshape(6, owners, depth), 0, 1).reshape(owners, -1)
    g_out = owned(dot(d_attn, mixed_rows, TN))
    d_query, d_kv, d_far = attention_call(
        attend_back_kernel, "attend_back", queries, kv, kv_far, [d_mixed], [logs],
        ["row", "pair", "far"], 5, head,
    )
    d_kv = (d_kv + lax.ppermute(d_far, "seq", swap).astype(F32)).astype(BF16)
    d_qkv = jnp.concatenate([d_query, d_kv[0], d_kv[1]], -1).reshape(micro * rows, 3 * cols)
    partial = dot(d_qkv, qkv_weights, NT).astype(BF16).reshape(micro, n, own, width)
    sums = jnp.sum(d_qkv.astype(F32), 0).reshape(3, heads_here, owners, head // owners)
    g_bqv = jnp.moveaxis(jnp.stack([sums[0], sums[2]]), 2, 0).reshape(owners, -1)
    g_small = owned_small(jnp.concatenate([g_bqv, norm_sums], 1))
    g_qkv = owned(dot(gathered, d_qkv, TN))
    d_inputs, g_out, g_qkv, g_small = exchange(
        n, "input_grad", 4, work_last, partial, [d_first], [(piece, BF16)], False, piece,
        grads=[g_out, g_qkv, g_small],
    )

    g_small = g_small.reshape(-1)
    bqv_grad = g_small[: b_qv.size].reshape(b_qv.shape)
    norm_mine = g_small[b_qv.size : b_qv.size + 6 * depth].reshape(6, depth)
    gain_grad = jnp.stack([norm_mine[0], norm_mine[3]])
    shift_grad = jnp.stack([norm_mine[1], norm_mine[2], norm_mine[4], norm_mine[5]])
    qkv_grad = jnp.swapaxes(g_qkv.reshape(depth, 3, cols), 0, 1)
    bup_grad = g_bup.reshape(-1)[: b_up.size].reshape(b_up.shape)
    return (
        result[:, None],
        d_inputs[:, None],
        qkv_grad,
        bqv_grad,
        g_out.T,
        g_up,
        bup_grad,
        g_down.T,
        gain_grad,
        shift_grad,
    )


def solution(mesh):
    rows_spec = P(None, "dp", ("seq", "heads"), None)
    weight_specs = (
        P(None, ("dp", "seq"), "heads"),
        P(None, "heads", ("dp", "seq")),
        P("heads", ("dp", "seq")),
        P(("dp", "seq"), "heads"),
        P("heads", ("dp", "seq")),
        P("heads", ("dp", "seq")),
        P(None, ("dp", "seq")),
        P(None, ("dp", "seq")),
    )
    return jax.shard_map(
        local,
        mesh=mesh,
        in_specs=(rows_spec,) + weight_specs + (rows_spec,),
        out_specs=(rows_spec, rows_spec) + weight_specs,
        check_vma=False,
    )
```

```python
import functools

import jax
import jax.numpy as jnp
from jax import lax
from jax.experimental import pallas as pl
from jax.experimental.pallas import tpu as pltpu
from jax.sharding import PartitionSpec as P

EPSILON = 1e-05
F32 = jnp.float32
BF16 = jnp.bfloat16
MESH = pl.DeviceIdType.MESH
VMEM_SPEC = pl.BlockSpec(memory_space=pltpu.VMEM)
VMEM_LIMIT = 48 * 1024 * 1024


def dot(left, right, dims):
    return lax.dot_general(left, right, (dims, ((), ())), preferred_element_type=F32)


NN = ((1,), (0,))
NT = ((1,), (1,))
TN = ((0,), (0,))


def norm_parts(rows):
    centred = rows - jnp.mean(rows, -1, keepdims=True)
    spread = jnp.mean(centred * centred, -1, keepdims=True)
    scale = lax.rsqrt(spread + EPSILON)
    return centred * scale, scale


def norm_back(grad, unit, scale, gain):
    inner = grad * gain
    mean_one = jnp.mean(inner, -1, keepdims=True)
    mean_two = jnp.mean(inner * unit, -1, keepdims=True)
    return scale * (inner - mean_one - unit * mean_two)


def row_sum(rows):
    return jnp.sum(rows, 0, keepdims=True)


def exchange_kernel(n, far, parts, has_sum, has_send, tail, work, n_in, n_out, n_grad, n_spread, *refs):
    refs = list(refs)
    partial = refs.pop(0) if has_sum else None
    ins = [refs.pop(0) for _ in range(n_in)]
    grads = [refs.pop(0) for _ in range(n_grad)]
    spread = [refs.pop(0) for _ in range(n_spread)]
    gathered = refs.pop(0) if has_send else None
    outs = [refs.pop(0) for _ in range(n_out)]
    grad_outs = [refs.pop(0) for _ in range(n_grad)]
    spread_outs = [refs.pop(0) for _ in range(n_spread)]
    relay = n == 4
    if has_sum:
        landing, sum_send, sum_recv = refs.pop(0), refs.pop(0), refs.pop(0)
        if relay:
            relay_in, relay_out, relay_send, relay_recv = [refs.pop(0) for _ in range(4)]
    if has_send:
        all_send, all_recv = refs.pop(0), refs.pop(0)
    if tail:
        tail_land, tail_send, tail_recv = refs.pop(0), refs.pop(0), refs.pop(0)
    grad_scratch = [[refs.pop(0) for _ in range(6)] for _ in range(n_grad)]
    spread_sems = [[refs.pop(0), refs.pop(0)] for _ in range(n_spread)]
    me = lax.axis_index("heads")

    def start_at(src, dst, send_sem, recv_sem, target):
        copy = pltpu.make_async_remote_copy(
            src_ref=src,
            dst_ref=dst,
            send_sem=send_sem,
            recv_sem=recv_sem,
            device_id=target,
            device_id_type=MESH,
        )
        copy.start()
        return copy

    def start(src, dst, send_sem, recv_sem, k):
        return start_at(src, dst, send_sem, recv_sem, {"heads": me ^ k})

    barrier = pltpu.get_barrier_semaphore()
    for k in range(1, n):
        pl.semaphore_signal(barrier, inc=1, device_id={"heads": me ^ k}, device_id_type=MESH)
    side = lax.axis_index("seq")
    place = lax.axis_index("dp")
    ahead = [lax.rem(place + j, far) for j in range(far)]
    owners = []
    if n_grad:
        owners = [{"seq": 1 - side}] + [{"dp": ahead[j]} for j in range(1, far)]
    if n_spread:
        owners = [
            {"dp": ahead[j], "seq": 1 - side if c else side}
            for j in range(far)
            for c in (0, 1)
            if j or c
        ]
    for target in owners:
        pl.semaphore_signal(barrier, inc=1, device_id=target, device_id_type=MESH)
    pl.semaphore_wait(barrier, n - 1 + len(owners))

    spread_copies = []
    mine = 2 * place + side
    for src, dst, sems in zip(spread, spread_outs, spread_sems):
        for at, target in enumerate(owners):
            spread_copies.append(
                start_at(src.at[...], dst.at[mine], sems[0].at[at], sems[1].at[at], target)
            )
        dst[mine] = src[...]

    core_copies, far_copies = {}, {}
    for at, (ref, scratch) in enumerate(zip(grads, grad_scratch)):
        for j in list(range(1, far)) + [0]:
            core_copies[at, j] = start_at(
                ref.at[2 * ahead[j] + 1 - side],
                scratch[0].at[ahead[j]],
                scratch[2].at[j],
                scratch[3].at[j],
                {"seq": 1 - side},
            )

    own = (partial if has_sum else gathered).shape[2]
    halves = (pl.ds(0, own // 2), pl.ds(own // 2, own // 2))
    started = []
    sums = {}
    relays = {}
    if has_sum and relay:
        for part in range(parts):
            for k in (1, 2):
                relays[part, k] = start(
                    partial.at[part, me ^ 3, halves[k - 1]],
                    relay_in.at[part, k - 1],
                    relay_send.at[part, k - 1],
                    relay_recv.at[part, k - 1],
                    k,
                )
            for k in (1, 2):
                half = halves[k - 1]
                sums[part, k, 0] = start(
                    partial.at[part, me ^ k, half],
                    landing.at[part, k - 1, half],
                    sum_send.at[part, k - 1],
                    sum_recv.at[part, k - 1],
                    k,
                )
    for at, (ref, scratch) in enumerate(zip(grads, grad_scratch)):
        for j in range(1, far):
            core_copies[at, j].wait_recv()
            scratch[0][ahead[j]] = (
                ref[2 * ahead[j] + side].astype(F32) + scratch[0][ahead[j]].astype(F32)
            ).astype(ref.dtype)
            far_copies[at, j] = start_at(
                scratch[0].at[ahead[j]],
                scratch[1].at[j - 1],
                scratch[4].at[j - 1],
                scratch[5].at[j - 1],
                {"dp": ahead[j]},
            )
    if has_sum and relay:
        for part in range(parts):
            for k in (1, 2):
                other, half = 3 - k, halves[k - 1]
                relays[part, k].wait_recv()
                relay_out[part, k - 1] = (
                    partial[part, me ^ other, half].astype(F32)
                    + relay_in[part, k - 1].astype(F32)
                ).astype(BF16)
                sums[part, other, 1] = start(
                    relay_out.at[part, k - 1],
                    landing.at[part, other - 1, half],
                    sum_send.at[part, 1 + other],
                    sum_recv.at[part, 1 + other],
                    other,
                )
    if has_sum and not relay:
        for part in range(parts):
            for k in range(1, n):
                sums[part, k, 0] = start(
                    partial.at[part, me ^ k],
                    landing.at[part, k - 1],
                    sum_send.at[part, k - 1],
                    sum_recv.at[part, k - 1],
                    k,
                )
    neighbours = (1, 2) if relay else tuple(range(1, n))
    sends = {}
    for part in range(parts):
        total = None
        if has_sum:
            total = partial[part, me].astype(F32)
            for k in neighbours:
                sums[part, k, 0].wait_recv()
                if relay:
                    sums[part, k, 1].wait_recv()
                total = total + landing[part, k - 1].astype(F32)
        passed = work(part, total, ins, outs)
        if has_send:
            gathered[part, me] = passed
            for k in neighbours:
                sends[part, k] = start(
                    gathered.at[part, me],
                    gathered.at[part, me],
                    all_send.at[part, k - 1],
                    all_recv.at[part, k - 1],
                    k,
                )
    if tail:
        mine = [sum(ref[part] for part in range(parts)) for ref in (outs[1], ins[-1])]
        tail_land[me] = jnp.concatenate(mine + [jnp.zeros((2, mine[0].shape[1]), F32)], 0)
        tails = [
            start(tail_land.at[me], tail_land.at[me], tail_send.at[k - 1], tail_recv.at[k - 1], k)
            for k in range(1, n)
        ]
    if has_send and relay:
        for part in range(parts):
            for k in (1, 2):
                sends[part, k].wait_recv()
                half = halves[k - 1]
                other = 3 - k
                started.append(
                    start(
                        gathered.at[part, me ^ k, half],
                        gathered.at[part, me ^ k, half],
                        all_send.at[part, 1 + other],
                        all_recv.at[part, 1 + other],
                        other,
                    )
                )
        for copy in started:
            copy.wait_recv()
    elif has_send:
        for copy in sends.values():
            copy.wait_recv()
    if tail:
        for copy in tails:
            copy.wait_recv()
        outs[-1][...] = sum(tail_land[k, 0:6] for k in range(n))
        for copy in tails:
            copy.wait_send()
    for at, (ref, scratch) in enumerate(zip(grads, grad_scratch)):
        core_copies[at, 0].wait_recv()
        total = ref[2 * place + side].astype(F32) + scratch[0][place].astype(F32)
        for j in range(1, far):
            far_copies[at, j].wait_recv()
            total = total + scratch[1][j - 1].astype(F32)
        grad_outs[at][...] = total
    for copy in spread_copies:
        copy.wait()
    started += list(core_copies.values()) + list(far_copies.values())
    for copy in list(relays.values()) + list(sums.values()) + list(sends.values()) + started:
        copy.wait_send()


def exchange(n, name, ident, work, partial, ins, out_shapes, has_send, shape, tail=False, grads=(), spread=()):
    parts, rows, width = shape
    has_sum = partial is not None
    relay = n == 4
    far = lax.axis_size("dp")
    operands = ([partial] if has_sum else []) + list(ins) + list(grads) + list(spread)
    shapes = ([jax.ShapeDtypeStruct((parts, n, rows, width), BF16)] if has_send else []) + [
        jax.ShapeDtypeStruct(s, t) for s, t in out_shapes
    ]
    shapes += [jax.ShapeDtypeStruct(g.shape[1:], F32) for g in grads]
    shapes += [jax.ShapeDtypeStruct((2 * far,) + v.shape, v.dtype) for v in spread]
    sems = pltpu.SemaphoreType.DMA((parts, 4 if relay else n - 1))
    scratch = []
    if has_sum:
        scratch += [pltpu.VMEM((parts, 2 if relay else n - 1, rows, width), BF16), sems, sems]
        if relay:
            scratch += [pltpu.VMEM((parts, 2, rows // 2, width), BF16)] * 2
            scratch += [pltpu.SemaphoreType.DMA((parts, 2))] * 2
    if has_send:
        scratch += [sems, sems]
    if tail:
        scratch += [pltpu.VMEM((n, 8, width), F32)] + [pltpu.SemaphoreType.DMA((n - 1,))] * 2
    for g in grads:
        scratch += [pltpu.VMEM((count,) + g.shape[1:], g.dtype) for count in (far, far - 1)]
        scratch += [pltpu.SemaphoreType.DMA((far,))] * 2 + [pltpu.SemaphoreType.DMA((far - 1,))] * 2
    for _ in spread:
        scratch += [pltpu.SemaphoreType.DMA((2 * far - 1,))] * 2
    return pl.pallas_call(
        functools.partial(
            exchange_kernel, n, far, parts, has_sum, has_send, tail, work, len(ins),
            len(out_shapes), len(grads), len(spread),
        ),
        out_shape=shapes,
        in_specs=[VMEM_SPEC] * len(operands),
        out_specs=[VMEM_SPEC] * len(shapes),
        scratch_shapes=scratch,
        compiler_params=pltpu.CompilerParams(
            collective_id=ident, has_side_effects=True, vmem_limit_bytes=VMEM_LIMIT
        ),
        cost_estimate=pl.CostEstimate(
            flops=1000000, bytes_accessed=60000000, transcendentals=0
        ),
        name=name,
    )(*operands)


def work_inputs(part, total, ins, outs):
    return ins[0][part]


def work_first(part, total, ins, outs):
    x_rows, gains, shifts = ins
    first = x_rows[part].astype(F32) + total + shifts[0:1]
    outs[0][part] = first
    unit, _ = norm_parts(first)
    normed = (unit * gains[0:1] + shifts[1:2]).astype(BF16)
    outs[1][part] = normed
    return normed


def work_second(part, total, ins, outs):
    normed, cotangent, gains, shifts = ins
    second = normed[part].astype(F32) + total + shifts[2:3]
    unit, scale = norm_parts(second)
    outs[0][part] = (unit * gains[1:2] + shifts[3:4]).astype(BF16)
    grad = cotangent[part].astype(F32)
    d_second = norm_back(grad, unit, scale, gains[1:2])
    outs[1][part] = d_second
    low = d_second.astype(BF16)
    sums = jnp.concatenate(
        [row_sum(grad * unit), row_sum(low.astype(F32)), row_sum(grad)], 0
    )
    outs[2][part] = sums
    return low


def work_third(part, total, ins, outs):
    first, d_second, gains, _ = ins
    grad = total + d_second[part]
    unit, scale = norm_parts(first[part])
    d_first = norm_back(grad, unit, scale, gains[0:1])
    outs[0][part] = d_first
    low = d_first.astype(BF16)
    sums = jnp.concatenate(
        [row_sum(grad * unit), row_sum(low.astype(F32)), row_sum(grad)], 0
    )
    outs[1][part] = sums
    return low


def work_last(part, total, ins, outs):
    outs[0][part] = (total + ins[0][part]).astype(BF16)
    return None


def attend_kernel(head, q_ref, k_ref, v_ref, k_far, v_far, o_ref, log_ref):
    queries = q_ref[0] * jnp.asarray(0.125, BF16)
    keys = jnp.concatenate([k_ref[0], k_far[0]], 0)
    values = jnp.concatenate([v_ref[0], v_far[0]], 0)
    mixed, logs = [], []
    for h in range(q_ref.shape[-1] // head):
        cols = slice(h * head, (h + 1) * head)
        scores = dot(keys[:, cols], queries[:, cols], NT)
        largest = jnp.max(scores, 0, keepdims=True)
        weights = jnp.exp(scores - largest)
        totals = jnp.sum(weights, 0, keepdims=True)
        probs = (weights * (1.0 / totals)).astype(BF16)
        mixed.append(dot(probs, values[:, cols], TN))
        logs.append(largest + jnp.log(totals))
    o_ref[0] = jnp.concatenate(mixed, -1).astype(BF16)
    log_ref[0, 0] = jnp.concatenate(logs, 0)


def attend_back_kernel(
    head, q_ref, k_ref, v_ref, k_far, v_far, do_ref, log_ref, dq_ref, dkv_ref, far_ref
):
    half = k_ref.shape[1]
    queries = q_ref[0] * jnp.asarray(0.125, BF16)
    keys = jnp.concatenate([k_ref[0], k_far[0]], 0)
    values = jnp.concatenate([v_ref[0], v_far[0]], 0)
    d_mixed = do_ref[0]
    dq, dk, dv = [], [], []
    for h in range(q_ref.shape[-1] // head):
        cols = slice(h * head, (h + 1) * head)
        scores = dot(keys[:, cols], queries[:, cols], NT)
        probs = jnp.exp(scores - log_ref[0, 0, h : h + 1])
        d_probs = dot(values[:, cols], d_mixed[:, cols], NT)
        centre = jnp.sum(probs * d_probs, 0, keepdims=True)
        d_scores = (probs * (d_probs - centre)).astype(BF16)
        dv.append(dot(probs.astype(BF16), d_mixed[:, cols], NN))
        dk.append(dot(d_scores, queries[:, cols], NN))
        dq.append(dot(d_scores, keys[:, cols], TN) * 0.125)
    dq_ref[0] = jnp.concatenate(dq, -1).astype(BF16)
    for at, rows in enumerate((dk, dv)):
        rows = jnp.concatenate(rows, -1)
        dkv_ref[at, 0] = rows[:half]
        far_ref[at, 0] = rows[half:].astype(BF16)


def attention_call(kernel, name, queries, kv, kv_far, more, more_logs, outs, dots, head):
    micro, rows, width = queries.shape
    half = kv.shape[1]
    block = min(128, width)
    blocks = width // block
    row_spec = pl.BlockSpec((1, rows, block), lambda m, j: (m, 0, j))
    log_spec = pl.BlockSpec((1, 1, block // head, rows), lambda m, j: (m, j, 0, 0))
    pair_spec = pl.BlockSpec((2, 1, half, block), lambda m, j: (0, m, 0, j))
    shared = block % 128 == 0
    skip = blocks if shared else 0
    value_spec = pl.BlockSpec((1, half, block), lambda m, j: (m, 0, j + skip))
    both = [(v, v) if shared else (v[..., :width], v[..., width:]) for v in (kv, kv_far)]
    kinds = {
        "row": (row_spec, jax.ShapeDtypeStruct(queries.shape, BF16)),
        "log": (log_spec, jax.ShapeDtypeStruct((micro, blocks, block // head, rows), F32)),
        "pair": (pair_spec, jax.ShapeDtypeStruct((2, micro, half, width), F32)),
        "far": (pair_spec, jax.ShapeDtypeStruct((2, micro, half, width), BF16)),
    }
    return pl.pallas_call(
        functools.partial(kernel, head),
        grid=(micro, blocks),
        in_specs=[row_spec] + [row_spec, value_spec] * 2
        + [row_spec] * len(more) + [log_spec] * len(more_logs),
        out_specs=[kinds[k][0] for k in outs],
        out_shape=[kinds[k][1] for k in outs],
        compiler_params=pltpu.CompilerParams(vmem_limit_bytes=VMEM_LIMIT),
        cost_estimate=pl.CostEstimate(
            flops=2 * dots * micro * rows * 2 * half * width * 4,
            bytes_accessed=20000000,
            transcendentals=0,
        ),
        name=name,
    )(queries, *both[0], *both[1], *more, *more_logs)


def gelu_parts(value):
    cdf = 0.5 * (1.0 + lax.erf(value * 0.7071067811865476))
    return cdf, 0.3989422804014327 * jnp.exp(-0.5 * value * value)


def local(inputs, w_qkv, b_qv, w_out, w_up, b_up, w_down, ln_gains, ln_shifts, cotangent):
    n = lax.axis_size("heads")
    owners = lax.axis_size("dp") * lax.axis_size("seq")
    share = ("dp", "seq")
    micro, _, own, width = inputs.shape
    rows = n * own
    heads_here, head = b_qv.shape[1], b_qv.shape[2] * owners
    cols = heads_here * head
    depth = w_qkv.shape[1]
    hidden_here = w_up.shape[1]
    piece = (micro, own, width)

    qkv_mine = jnp.concatenate([w_qkv[0], w_qkv[1], w_qkv[2]], 1)
    qkv_weights = lax.all_gather(qkv_mine, share, axis=0, tiled=True)
    small = jnp.concatenate([v.reshape(-1) for v in (b_qv, b_up, ln_gains, ln_shifts)])
    small = jnp.pad(small, (0, -small.size % (16 * 128))).reshape(16, -1)
    x_rows = inputs[:, 0]
    gathered, small_all, out_all = exchange(
        n, "gather_inputs", 0, work_inputs, None, [x_rows], [], True, piece,
        spread=[small, w_out.T],
    )
    out_all = out_all.reshape(owners * depth, cols)
    gathered = gathered.reshape(micro * rows, width)
    up_all = lax.all_gather(w_up, share, axis=0, tiled=True)
    down_all = lax.all_gather(w_down.T, share, axis=0, tiled=True)

    q_weights = qkv_weights[:, :cols]
    kv_weights = qkv_weights[:, cols:]
    small_all = small_all.reshape(owners, -1)
    at = 0
    pieces = []
    for v in (b_qv, b_up, ln_gains, ln_shifts):
        part = small_all[:, at : at + v.size].reshape((owners,) + v.shape)
        pieces.append(jnp.moveaxis(part, 0, -2).reshape(v.shape[:-1] + (-1,)).astype(F32))
        at += v.size
    bias_qv, bias_up, gains, shifts = pieces
    bias_qv = bias_qv.reshape(2, cols)
    bias_kv = jnp.concatenate([jnp.zeros_like(bias_qv[0]), bias_qv[1]])
    swap = [(0, 1), (1, 0)]

    kv = (dot(gathered, kv_weights, NN) + bias_kv).astype(BF16).reshape(micro, rows, 2 * cols)
    kv_far = lax.ppermute(kv, "seq", swap)
    queries = (dot(gathered, q_weights, NN) + bias_qv[0]).astype(BF16).reshape(micro, rows, cols)
    mixed, logs = attention_call(
        attend_kernel, "attend", queries, kv, kv_far, [], [], ["row", "log"], 2, head
    )
    mixed_rows = mixed.reshape(micro * rows, cols)
    partial = dot(mixed_rows, out_all, NT).astype(BF16).reshape(micro, n, own, width)
    normed_all, first, normed = exchange(
        n, "first_norm", 1, work_first, partial, [x_rows, gains, shifts],
        [(piece, F32), (piece, BF16)], True, piece,
    )
    normed_all = normed_all.reshape(micro * rows, width)
    hidden_pre = dot(normed_all, up_all, NN) + bias_up.reshape(-1)
    cdf, density = gelu_parts(hidden_pre)
    hidden = (hidden_pre * cdf).astype(BF16)
    slope = cdf + hidden_pre * density
    partial = dot(hidden, down_all, NT).astype(BF16).reshape(micro, n, own, width)
    d_mlp, result, d_second, sums_two = exchange(
        n, "second_norm", 2, work_second, partial, [normed, cotangent[:, 0], gains, shifts],
        [(piece, BF16), (piece, F32), ((micro, 3, width), F32)], True, piece,
    )

    d_mlp = d_mlp.reshape(micro * rows, width)
    d_pre_wide = dot(d_mlp, down_all, NN) * slope
    d_pre = d_pre_wide.astype(BF16)
    partial = dot(d_pre, up_all, NT).astype(BF16).reshape(micro, n, own, width)
    def owned(wide):
        return wide.astype(BF16).reshape(owners, -1, wide.shape[-1])

    def owned_small(values):
        return jnp.pad(values, ((0, 0), (0, -values.shape[-1] % 1024))).reshape(owners, 8, -1)

    g_down = owned(dot(d_mlp, hidden, TN))
    g_up = owned(dot(normed_all, d_pre, TN))
    g_bup = jnp.sum(d_pre.astype(F32), 0).reshape(b_up.shape[0], owners, b_up.shape[1])
    g_bup = owned_small(jnp.swapaxes(g_bup, 0, 1).reshape(owners, -1))
    partial, g_down = lax.optimization_barrier((partial, g_down))
    g_down = lax.psum_scatter(g_down, share, scatter_dimension=0, tiled=False)
    d_attn, d_first, _, norm_sums, g_up, g_bup = exchange(
        n, "first_norm_back", 3, work_third, partial, [first, d_second, gains, sums_two],
        [(piece, F32), ((micro, 3, width), F32), ((6, width), F32)], True, piece, tail=True,
        grads=[g_up, g_bup],
    )

    d_attn = d_attn.reshape(micro * rows, width)
    d_mixed = dot(d_attn, out_all, NN).astype(BF16).reshape(micro, rows, cols)
    norm_sums = jnp.swapaxes(norm_sums.reshape(6, owners, depth), 0, 1).reshape(owners, -1)
    g_out = owned(dot(d_attn, mixed_rows, TN))
    d_mixed, g_down = lax.optimization_barrier((d_mixed, g_down))
    d_query, d_kv, d_far = attention_call(
        attend_back_kernel, "attend_back", queries, kv, kv_far, [d_mixed], [logs],
        ["row", "pair", "far"], 5, head,
    )
    d_kv = (d_kv + lax.ppermute(d_far, "seq", swap).astype(F32)).astype(BF16)
    d_qkv = jnp.concatenate([d_query, d_kv[0], d_kv[1]], -1).reshape(micro * rows, 3 * cols)
    partial = dot(d_qkv, qkv_weights, NT).astype(BF16).reshape(micro, n, own, width)
    sums = jnp.sum(d_qkv.astype(F32), 0).reshape(3, heads_here, owners, head // owners)
    g_bqv = jnp.moveaxis(jnp.stack([sums[0], sums[2]]), 2, 0).reshape(owners, -1)
    g_small = owned_small(jnp.concatenate([g_bqv, norm_sums], 1))
    g_qkv = owned(dot(gathered, d_qkv, TN))
    d_inputs, g_out, g_qkv, g_small = exchange(
        n, "input_grad", 4, work_last, partial, [d_first], [(piece, BF16)], False, piece,
        grads=[g_out, g_qkv, g_small],
    )

    g_small = g_small.reshape(-1)
    bqv_grad = g_small[: b_qv.size].reshape(b_qv.shape)
    norm_mine = g_small[b_qv.size : b_qv.size + 6 * depth].reshape(6, depth)
    gain_grad = jnp.stack([norm_mine[0], norm_mine[3]])
    shift_grad = jnp.stack([norm_mine[1], norm_mine[2], norm_mine[4], norm_mine[5]])
    qkv_grad = jnp.swapaxes(g_qkv.reshape(depth, 3, cols), 0, 1)
    bup_grad = g_bup.reshape(-1)[: b_up.size].reshape(b_up.shape)
    return (
        result[:, None],
        d_inputs[:, None],
        qkv_grad,
        bqv_grad,
        g_out.T,
        g_up,
        bup_grad,
        g_down.astype(F32).T,
        gain_grad,
        shift_grad,
    )


def solution(mesh):
    rows_spec = P(None, "dp", ("seq", "heads"), None)
    weight_specs = (
        P(None, ("dp", "seq"), "heads"),
        P(None, "heads", ("dp", "seq")),
        P("heads", ("dp", "seq")),
        P(("dp", "seq"), "heads"),
        P("heads", ("dp", "seq")),
        P("heads", ("dp", "seq")),
        P(None, ("dp", "seq")),
        P(None, ("dp", "seq")),
    )
    return jax.shard_map(
        local,
        mesh=mesh,
        in_specs=(rows_spec,) + weight_specs + (rows_spec,),
        out_specs=(rows_spec, rows_spec) + weight_specs,
        check_vma=False,
    )
```

```python
import functools

import jax
import jax.numpy as jnp
from jax import lax
from jax.experimental import pallas as pl
from jax.experimental.pallas import tpu as pltpu
from jax.sharding import PartitionSpec as P

EPSILON = 1e-05
F32 = jnp.float32
BF16 = jnp.bfloat16
MESH = pl.DeviceIdType.MESH
VMEM_SPEC = pl.BlockSpec(memory_space=pltpu.VMEM)
VMEM_LIMIT = 48 * 1024 * 1024


def dot(left, right, dims):
    return lax.dot_general(left, right, (dims, ((), ())), preferred_element_type=F32)


NN = ((1,), (0,))
NT = ((1,), (1,))
TN = ((0,), (0,))


def norm_parts(rows):
    centred = rows - jnp.mean(rows, -1, keepdims=True)
    spread = jnp.mean(centred * centred, -1, keepdims=True)
    scale = lax.rsqrt(spread + EPSILON)
    return centred * scale, scale


def norm_back(grad, unit, scale, gain):
    inner = grad * gain
    mean_one = jnp.mean(inner, -1, keepdims=True)
    mean_two = jnp.mean(inner * unit, -1, keepdims=True)
    return scale * (inner - mean_one - unit * mean_two)


def row_sum(rows):
    return jnp.sum(rows, 0, keepdims=True)


def exchange_kernel(n, far, parts, has_sum, has_send, tail, work, n_in, n_out, n_grad, n_spread, *refs):
    refs = list(refs)
    partial = refs.pop(0) if has_sum else None
    ins = [refs.pop(0) for _ in range(n_in)]
    grads = [refs.pop(0) for _ in range(n_grad)]
    spread = [refs.pop(0) for _ in range(n_spread)]
    gathered = refs.pop(0) if has_send else None
    outs = [refs.pop(0) for _ in range(n_out)]
    grad_outs = [refs.pop(0) for _ in range(n_grad)]
    spread_outs = [refs.pop(0) for _ in range(n_spread)]
    relay = n == 4
    if has_sum:
        landing, sum_send, sum_recv = refs.pop(0), refs.pop(0), refs.pop(0)
        if relay:
            relay_in, relay_out, relay_send, relay_recv = [refs.pop(0) for _ in range(4)]
    if has_send:
        all_send, all_recv = refs.pop(0), refs.pop(0)
    if tail:
        tail_land, tail_send, tail_recv = refs.pop(0), refs.pop(0), refs.pop(0)
    grad_scratch = [[refs.pop(0) for _ in range(6)] for _ in range(n_grad)]
    spread_sems = [[refs.pop(0), refs.pop(0)] for _ in range(n_spread)]
    me = lax.axis_index("heads")

    def start_at(src, dst, send_sem, recv_sem, target):
        copy = pltpu.make_async_remote_copy(
            src_ref=src,
            dst_ref=dst,
            send_sem=send_sem,
            recv_sem=recv_sem,
            device_id=target,
            device_id_type=MESH,
        )
        copy.start()
        return copy

    def start(src, dst, send_sem, recv_sem, k):
        return start_at(src, dst, send_sem, recv_sem, {"heads": me ^ k})

    barrier = pltpu.get_barrier_semaphore()
    for k in range(1, n):
        pl.semaphore_signal(barrier, inc=1, device_id={"heads": me ^ k}, device_id_type=MESH)
    side = lax.axis_index("seq")
    place = lax.axis_index("dp")
    ahead = [lax.rem(place + j, far) for j in range(far)]
    owners = []
    if n_grad or n_spread:
        owners = [{"seq": 1 - side}] + [{"dp": ahead[j]} for j in range(1, far)]
    for target in owners:
        pl.semaphore_signal(barrier, inc=1, device_id=target, device_id_type=MESH)
    pl.semaphore_wait(barrier, n - 1 + len(owners))

    spread_copies = {}
    mine = 2 * place + side
    for at, (src, dst, sems) in enumerate(zip(spread, spread_outs, spread_sems)):
        for j in range(far):
            spread_copies[at, j] = start_at(
                src.at[...],
                dst.at[mine],
                sems[0].at[j],
                sems[1].at[j],
                {"dp": ahead[j]} if j else {"seq": 1 - side},
            )
        dst[mine] = src[...]

    core_copies, far_copies = {}, {}
    for at, (ref, scratch) in enumerate(zip(grads, grad_scratch)):
        for j in list(range(1, far)) + [0]:
            core_copies[at, j] = start_at(
                ref.at[2 * ahead[j] + 1 - side],
                scratch[0].at[ahead[j]],
                scratch[2].at[j],
                scratch[3].at[j],
                {"seq": 1 - side},
            )

    own = (partial if has_sum else gathered).shape[2]
    halves = (pl.ds(0, own // 2), pl.ds(own // 2, own // 2))
    started = []
    sums = {}
    relays = {}
    if has_sum and relay:
        for part in range(parts):
            for k in (1, 2):
                relays[part, k] = start(
                    partial.at[part, me ^ 3, halves[k - 1]],
                    relay_in.at[part, k - 1],
                    relay_send.at[part, k - 1],
                    relay_recv.at[part, k - 1],
                    k,
                )
            for k in (1, 2):
                half = halves[k - 1]
                sums[part, k, 0] = start(
                    partial.at[part, me ^ k, half],
                    landing.at[part, k - 1, half],
                    sum_send.at[part, k - 1],
                    sum_recv.at[part, k - 1],
                    k,
                )
    for at, (ref, scratch) in enumerate(zip(grads, grad_scratch)):
        for j in range(1, far):
            core_copies[at, j].wait_recv()
            scratch[0][ahead[j]] = (
                ref[2 * ahead[j] + side].astype(F32) + scratch[0][ahead[j]].astype(F32)
            ).astype(ref.dtype)
            far_copies[at, j] = start_at(
                scratch[0].at[ahead[j]],
                scratch[1].at[j - 1],
                scratch[4].at[j - 1],
                scratch[5].at[j - 1],
                {"dp": ahead[j]},
            )
    if has_sum and relay:
        for part in range(parts):
            for k in (1, 2):
                other, half = 3 - k, halves[k - 1]
                relays[part, k].wait_recv()
                relay_out[part, k - 1] = (
                    partial[part, me ^ other, half].astype(F32)
                    + relay_in[part, k - 1].astype(F32)
                ).astype(BF16)
                sums[part, other, 1] = start(
                    relay_out.at[part, k - 1],
                    landing.at[part, other - 1, half],
                    sum_send.at[part, 1 + other],
                    sum_recv.at[part, 1 + other],
                    other,
                )
    if has_sum and not relay:
        for part in range(parts):
            for k in range(1, n):
                sums[part, k, 0] = start(
                    partial.at[part, me ^ k],
                    landing.at[part, k - 1],
                    sum_send.at[part, k - 1],
                    sum_recv.at[part, k - 1],
                    k,
                )
    neighbours = (1, 2) if relay else tuple(range(1, n))
    sends = {}
    for part in range(parts):
        total = None
        if has_sum:
            total = partial[part, me].astype(F32)
            for k in neighbours:
                sums[part, k, 0].wait_recv()
                if relay:
                    sums[part, k, 1].wait_recv()
                total = total + landing[part, k - 1].astype(F32)
        passed = work(part, total, ins, outs)
        if has_send:
            gathered[part, me] = passed
            for k in neighbours:
                sends[part, k] = start(
                    gathered.at[part, me],
                    gathered.at[part, me],
                    all_send.at[part, k - 1],
                    all_recv.at[part, k - 1],
                    k,
                )
    if tail:
        mine = [sum(ref[part] for part in range(parts)) for ref in (outs[1], ins[-1])]
        tail_land[me] = jnp.concatenate(mine + [jnp.zeros((2, mine[0].shape[1]), F32)], 0)
        tails = [
            start(tail_land.at[me], tail_land.at[me], tail_send.at[k - 1], tail_recv.at[k - 1], k)
            for k in range(1, n)
        ]
    if has_send and relay:
        for part in range(parts):
            for k in (1, 2):
                sends[part, k].wait_recv()
                half = halves[k - 1]
                other = 3 - k
                started.append(
                    start(
                        gathered.at[part, me ^ k, half],
                        gathered.at[part, me ^ k, half],
                        all_send.at[part, 1 + other],
                        all_recv.at[part, 1 + other],
                        other,
                    )
                )
        for copy in started:
            copy.wait_recv()
    elif has_send:
        for copy in sends.values():
            copy.wait_recv()
    if tail:
        for copy in tails:
            copy.wait_recv()
        outs[-1][...] = sum(tail_land[k, 0:6] for k in range(n))
        for copy in tails:
            copy.wait_send()
    for at, (ref, scratch) in enumerate(zip(grads, grad_scratch)):
        core_copies[at, 0].wait_recv()
        total = ref[2 * place + side].astype(F32) + scratch[0][place].astype(F32)
        for j in range(1, far):
            far_copies[at, j].wait_recv()
            total = total + scratch[1][j - 1].astype(F32)
        grad_outs[at][...] = total
    for at, (dst, sems) in enumerate(zip(spread_outs, spread_sems)):
        for j in range(1, far):
            spread_copies[at, j].wait_recv()
            slot = 2 * lax.rem(place + far - j, far) + side
            spread_copies[at, far + j] = start_at(
                dst.at[slot],
                dst.at[slot],
                sems[0].at[far - 1 + j],
                sems[1].at[far - 1 + j],
                {"seq": 1 - side},
            )
    for (_, j), copy in spread_copies.items():
        if j == 0 or j >= far:
            copy.wait_recv()
    started += list(spread_copies.values())
    started += list(core_copies.values()) + list(far_copies.values())
    for copy in list(relays.values()) + list(sums.values()) + list(sends.values()) + started:
        copy.wait_send()


def exchange(n, name, ident, work, partial, ins, out_shapes, has_send, shape, tail=False, grads=(), spread=()):
    parts, rows, width = shape
    has_sum = partial is not None
    relay = n == 4
    far = lax.axis_size("dp")
    operands = ([partial] if has_sum else []) + list(ins) + list(grads) + list(spread)
    shapes = ([jax.ShapeDtypeStruct((parts, n, rows, width), BF16)] if has_send else []) + [
        jax.ShapeDtypeStruct(s, t) for s, t in out_shapes
    ]
    shapes += [jax.ShapeDtypeStruct(g.shape[1:], F32) for g in grads]
    shapes += [jax.ShapeDtypeStruct((2 * far,) + v.shape, v.dtype) for v in spread]
    sems = pltpu.SemaphoreType.DMA((parts, 4 if relay else n - 1))
    scratch = []
    if has_sum:
        scratch += [pltpu.VMEM((parts, 2 if relay else n - 1, rows, width), BF16), sems, sems]
        if relay:
            scratch += [pltpu.VMEM((parts, 2, rows // 2, width), BF16)] * 2
            scratch += [pltpu.SemaphoreType.DMA((parts, 2))] * 2
    if has_send:
        scratch += [sems, sems]
    if tail:
        scratch += [pltpu.VMEM((n, 8, width), F32)] + [pltpu.SemaphoreType.DMA((n - 1,))] * 2
    for g in grads:
        scratch += [pltpu.VMEM((count,) + g.shape[1:], g.dtype) for count in (far, far - 1)]
        scratch += [pltpu.SemaphoreType.DMA((far,))] * 2 + [pltpu.SemaphoreType.DMA((far - 1,))] * 2
    for _ in spread:
        scratch += [pltpu.SemaphoreType.DMA((2 * far - 1,))] * 2
    return pl.pallas_call(
        functools.partial(
            exchange_kernel, n, far, parts, has_sum, has_send, tail, work, len(ins),
            len(out_shapes), len(grads), len(spread),
        ),
        out_shape=shapes,
        in_specs=[VMEM_SPEC] * len(operands),
        out_specs=[VMEM_SPEC] * len(shapes),
        scratch_shapes=scratch,
        compiler_params=pltpu.CompilerParams(
            collective_id=ident, has_side_effects=True, vmem_limit_bytes=VMEM_LIMIT
        ),
        cost_estimate=pl.CostEstimate(
            flops=1000000, bytes_accessed=60000000, transcendentals=0
        ),
        name=name,
    )(*operands)


def work_inputs(part, total, ins, outs):
    return ins[0][part]


def work_first(part, total, ins, outs):
    x_rows, gains, shifts = ins
    first = x_rows[part].astype(F32) + total + shifts[0:1]
    outs[0][part] = first
    unit, _ = norm_parts(first)
    normed = (unit * gains[0:1] + shifts[1:2]).astype(BF16)
    outs[1][part] = normed
    return normed


def work_second(part, total, ins, outs):
    normed, cotangent, gains, shifts = ins
    second = normed[part].astype(F32) + total + shifts[2:3]
    unit, scale = norm_parts(second)
    outs[0][part] = (unit * gains[1:2] + shifts[3:4]).astype(BF16)
    grad = cotangent[part].astype(F32)
    d_second = norm_back(grad, unit, scale, gains[1:2])
    outs[1][part] = d_second
    low = d_second.astype(BF16)
    sums = jnp.concatenate(
        [row_sum(grad * unit), row_sum(low.astype(F32)), row_sum(grad)], 0
    )
    outs[2][part] = sums
    return low


def work_third(part, total, ins, outs):
    first, d_second, gains, _ = ins
    grad = total + d_second[part]
    unit, scale = norm_parts(first[part])
    d_first = norm_back(grad, unit, scale, gains[0:1])
    outs[0][part] = d_first
    low = d_first.astype(BF16)
    sums = jnp.concatenate(
        [row_sum(grad * unit), row_sum(low.astype(F32)), row_sum(grad)], 0
    )
    outs[1][part] = sums
    return low


def work_last(part, total, ins, outs):
    outs[0][part] = (total + ins[0][part]).astype(BF16)
    return None


def attend_kernel(head, q_ref, k_ref, v_ref, k_far, v_far, o_ref, log_ref):
    queries = q_ref[0] * jnp.asarray(0.125, BF16)
    keys = jnp.concatenate([k_ref[0], k_far[0]], 0)
    values = jnp.concatenate([v_ref[0], v_far[0]], 0)
    mixed, logs = [], []
    for h in range(q_ref.shape[-1] // head):
        cols = slice(h * head, (h + 1) * head)
        scores = dot(keys[:, cols], queries[:, cols], NT)
        largest = jnp.max(scores, 0, keepdims=True)
        weights = jnp.exp(scores - largest)
        totals = jnp.sum(weights, 0, keepdims=True)
        probs = (weights * (1.0 / totals)).astype(BF16)
        mixed.append(dot(probs, values[:, cols], TN))
        logs.append(largest + jnp.log(totals))
    o_ref[0] = jnp.concatenate(mixed, -1).astype(BF16)
    log_ref[0, 0] = jnp.concatenate(logs, 0)


def attend_back_kernel(
    head, q_ref, k_ref, v_ref, k_far, v_far, do_ref, log_ref, dq_ref, dkv_ref, far_ref
):
    half = k_ref.shape[1]
    queries = q_ref[0] * jnp.asarray(0.125, BF16)
    keys = jnp.concatenate([k_ref[0], k_far[0]], 0)
    values = jnp.concatenate([v_ref[0], v_far[0]], 0)
    d_mixed = do_ref[0]
    dq, dk, dv = [], [], []
    for h in range(q_ref.shape[-1] // head):
        cols = slice(h * head, (h + 1) * head)
        scores = dot(keys[:, cols], queries[:, cols], NT)
        probs = jnp.exp(scores - log_ref[0, 0, h : h + 1])
        d_probs = dot(values[:, cols], d_mixed[:, cols], NT)
        centre = jnp.sum(probs * d_probs, 0, keepdims=True)
        d_scores = (probs * (d_probs - centre)).astype(BF16)
        dv.append(dot(probs.astype(BF16), d_mixed[:, cols], NN))
        dk.append(dot(d_scores, queries[:, cols], NN))
        dq.append(dot(d_scores, keys[:, cols], TN) * 0.125)
    dq_ref[0] = jnp.concatenate(dq, -1).astype(BF16)
    for at, rows in enumerate((dk, dv)):
        rows = jnp.concatenate(rows, -1)
        dkv_ref[at, 0] = rows[:half]
        far_ref[at, 0] = rows[half:].astype(BF16)


def attention_call(kernel, name, queries, kv, kv_far, more, more_logs, outs, dots, head):
    micro, rows, width = queries.shape
    half = kv.shape[1]
    block = min(128, width)
    blocks = width // block
    row_spec = pl.BlockSpec((1, rows, block), lambda m, j: (m, 0, j))
    log_spec = pl.BlockSpec((1, 1, block // head, rows), lambda m, j: (m, j, 0, 0))
    pair_spec = pl.BlockSpec((2, 1, half, block), lambda m, j: (0, m, 0, j))
    shared = block % 128 == 0
    skip = blocks if shared else 0
    value_spec = pl.BlockSpec((1, half, block), lambda m, j: (m, 0, j + skip))
    both = [(v, v) if shared else (v[..., :width], v[..., width:]) for v in (kv, kv_far)]
    kinds = {
        "row": (row_spec, jax.ShapeDtypeStruct(queries.shape, BF16)),
        "log": (log_spec, jax.ShapeDtypeStruct((micro, blocks, block // head, rows), F32)),
        "pair": (pair_spec, jax.ShapeDtypeStruct((2, micro, half, width), F32)),
        "far": (pair_spec, jax.ShapeDtypeStruct((2, micro, half, width), BF16)),
    }
    return pl.pallas_call(
        functools.partial(kernel, head),
        grid=(micro, blocks),
        in_specs=[row_spec] + [row_spec, value_spec] * 2
        + [row_spec] * len(more) + [log_spec] * len(more_logs),
        out_specs=[kinds[k][0] for k in outs],
        out_shape=[kinds[k][1] for k in outs],
        compiler_params=pltpu.CompilerParams(vmem_limit_bytes=VMEM_LIMIT),
        cost_estimate=pl.CostEstimate(
            flops=2 * dots * micro * rows * 2 * half * width * 4,
            bytes_accessed=20000000,
            transcendentals=0,
        ),
        name=name,
    )(queries, *both[0], *both[1], *more, *more_logs)


def gelu_parts(value):
    cdf = 0.5 * (1.0 + lax.erf(value * 0.7071067811865476))
    return cdf, 0.3989422804014327 * jnp.exp(-0.5 * value * value)


def local(inputs, w_qkv, b_qv, w_out, w_up, b_up, w_down, ln_gains, ln_shifts, cotangent):
    n = lax.axis_size("heads")
    owners = lax.axis_size("dp") * lax.axis_size("seq")
    share = ("dp", "seq")
    micro, _, own, width = inputs.shape
    rows = n * own
    heads_here, head = b_qv.shape[1], b_qv.shape[2] * owners
    cols = heads_here * head
    depth = w_qkv.shape[1]
    hidden_here = w_up.shape[1]
    piece = (micro, own, width)

    qkv_mine = jnp.concatenate([w_qkv[0], w_qkv[1], w_qkv[2]], 1)
    small = jnp.concatenate([v.reshape(-1) for v in (b_qv, b_up, ln_gains, ln_shifts)])
    small = jnp.pad(small, (0, -small.size % (16 * 128))).reshape(16, -1)
    x_rows = inputs[:, 0]
    gathered, small_all, out_all, qkv_weights = exchange(
        n, "gather_inputs", 0, work_inputs, None, [x_rows], [], True, piece,
        spread=[small, w_out.T, qkv_mine],
    )
    out_all = out_all.reshape(owners * depth, cols)
    qkv_weights = qkv_weights.reshape(owners * depth, 3 * cols)
    gathered = gathered.reshape(micro * rows, width)
    up_all = lax.all_gather(w_up, share, axis=0, tiled=True)
    down_all = lax.all_gather(w_down.T, share, axis=0, tiled=True)

    q_weights = qkv_weights[:, :cols]
    kv_weights = qkv_weights[:, cols:]
    small_all = small_all.reshape(owners, -1)
    at = 0
    pieces = []
    for v in (b_qv, b_up, ln_gains, ln_shifts):
        part = small_all[:, at : at + v.size].reshape((owners,) + v.shape)
        pieces.append(jnp.moveaxis(part, 0, -2).reshape(v.shape[:-1] + (-1,)).astype(F32))
        at += v.size
    bias_qv, bias_up, gains, shifts = pieces
    bias_qv = bias_qv.reshape(2, cols)
    bias_kv = jnp.concatenate([jnp.zeros_like(bias_qv[0]), bias_qv[1]])
    swap = [(0, 1), (1, 0)]

    kv = (dot(gathered, kv_weights, NN) + bias_kv).astype(BF16).reshape(micro, rows, 2 * cols)
    kv_far = lax.ppermute(kv, "seq", swap)
    queries = (dot(gathered, q_weights, NN) + bias_qv[0]).astype(BF16).reshape(micro, rows, cols)
    mixed, logs = attention_call(
        attend_kernel, "attend", queries, kv, kv_far, [], [], ["row", "log"], 2, head
    )
    mixed_rows = mixed.reshape(micro * rows, cols)
    partial = dot(mixed_rows, out_all, NT).astype(BF16).reshape(micro, n, own, width)
    normed_all, first, normed = exchange(
        n, "first_norm", 1, work_first, partial, [x_rows, gains, shifts],
        [(piece, F32), (piece, BF16)], True, piece,
    )
    normed_all = normed_all.reshape(micro * rows, width)
    hidden_pre = dot(normed_all, up_all, NN) + bias_up.reshape(-1)
    cdf, density = gelu_parts(hidden_pre)
    hidden = (hidden_pre * cdf).astype(BF16)
    slope = cdf + hidden_pre * density
    partial = dot(hidden, down_all, NT).astype(BF16).reshape(micro, n, own, width)
    d_mlp, result, d_second, sums_two = exchange(
        n, "second_norm", 2, work_second, partial, [normed, cotangent[:, 0], gains, shifts],
        [(piece, BF16), (piece, F32), ((micro, 3, width), F32)], True, piece,
    )

    d_mlp = d_mlp.reshape(micro * rows, width)
    d_pre_wide = dot(d_mlp, down_all, NN) * slope
    d_pre = d_pre_wide.astype(BF16)
    partial = dot(d_pre, up_all, NT).astype(BF16).reshape(micro, n, own, width)
    def owned(wide):
        return wide.astype(BF16).reshape(owners, -1, wide.shape[-1])

    def owned_small(values):
        return jnp.pad(values, ((0, 0), (0, -values.shape[-1] % 1024))).reshape(owners, 8, -1)

    g_down = owned(dot(d_mlp, hidden, TN))
    g_up = owned(dot(normed_all, d_pre, TN))
    g_bup = jnp.sum(d_pre.astype(F32), 0).reshape(b_up.shape[0], owners, b_up.shape[1])
    g_bup = owned_small(jnp.swapaxes(g_bup, 0, 1).reshape(owners, -1))
    partial, g_up = lax.optimization_barrier((partial, g_up))
    g_up = lax.psum_scatter(g_up, share, scatter_dimension=0, tiled=False)
    d_attn, d_first, _, norm_sums, g_down, g_bup = exchange(
        n, "first_norm_back", 3, work_third, partial, [first, d_second, gains, sums_two],
        [(piece, F32), ((micro, 3, width), F32), ((6, width), F32)], True, piece, tail=True,
        grads=[g_down, g_bup],
    )

    d_attn = d_attn.reshape(micro * rows, width)
    d_mixed = dot(d_attn, out_all, NN).astype(BF16).reshape(micro, rows, cols)
    norm_sums = jnp.swapaxes(norm_sums.reshape(6, owners, depth), 0, 1).reshape(owners, -1)
    g_out = owned(dot(d_attn, mixed_rows, TN))
    d_mixed, g_up = lax.optimization_barrier((d_mixed, g_up))
    d_query, d_kv, d_far = attention_call(
        attend_back_kernel, "attend_back", queries, kv, kv_far, [d_mixed], [logs],
        ["row", "pair", "far"], 5, head,
    )
    d_kv = (d_kv + lax.ppermute(d_far, "seq", swap).astype(F32)).astype(BF16)
    d_qkv = jnp.concatenate([d_query, d_kv[0], d_kv[1]], -1).reshape(micro * rows, 3 * cols)
    partial = dot(d_qkv, qkv_weights, NT).astype(BF16).reshape(micro, n, own, width)
    sums = jnp.sum(d_qkv.astype(F32), 0).reshape(3, heads_here, owners, head // owners)
    g_bqv = jnp.moveaxis(jnp.stack([sums[0], sums[2]]), 2, 0).reshape(owners, -1)
    g_small = owned_small(jnp.concatenate([g_bqv, norm_sums], 1))
    g_qkv = owned(dot(gathered, d_qkv, TN))
    d_inputs, g_out, g_qkv, g_small = exchange(
        n, "input_grad", 4, work_last, partial, [d_first], [(piece, BF16)], False, piece,
        grads=[g_out, g_qkv, g_small],
    )

    g_small = g_small.reshape(-1)
    bqv_grad = g_small[: b_qv.size].reshape(b_qv.shape)
    norm_mine = g_small[b_qv.size : b_qv.size + 6 * depth].reshape(6, depth)
    gain_grad = jnp.stack([norm_mine[0], norm_mine[3]])
    shift_grad = jnp.stack([norm_mine[1], norm_mine[2], norm_mine[4], norm_mine[5]])
    qkv_grad = jnp.swapaxes(g_qkv.reshape(depth, 3, cols), 0, 1)
    bup_grad = g_bup.reshape(-1)[: b_up.size].reshape(b_up.shape)
    return (
        result[:, None],
        d_inputs[:, None],
        qkv_grad,
        bqv_grad,
        g_out.T,
        g_up.astype(F32),
        bup_grad,
        g_down.T,
        gain_grad,
        shift_grad,
    )


def solution(mesh):
    rows_spec = P(None, "dp", ("seq", "heads"), None)
    weight_specs = (
        P(None, ("dp", "seq"), "heads"),
        P(None, "heads", ("dp", "seq")),
        P("heads", ("dp", "seq")),
        P(("dp", "seq"), "heads"),
        P("heads", ("dp", "seq")),
        P("heads", ("dp", "seq")),
        P(None, ("dp", "seq")),
        P(None, ("dp", "seq")),
    )
    return jax.shard_map(
        local,
        mesh=mesh,
        in_specs=(rows_spec,) + weight_specs + (rows_spec,),
        out_specs=(rows_spec, rows_spec) + weight_specs,
        check_vma=False,
    )
```
